512 devices in a mesh: hi: 16 (over z_lo, core), lo: 32 (over x, y, z_hi).
Axes of the slice: x: 4, y: 4, z: 16 (z_hi: 2, z_lo: 8; z = z_hi * 8 + z_lo), core: 2. Of those that a mesh axis runs over, the one named last changes fastest.
Arguments:
- fields: bfloat16 [2048, 2, 32, 128], P(('hi', 'lo')), may hold values from -6 to 6
- adjoint_in: bfloat16 [2048, 2, 32, 128], P(('hi', 'lo')), may hold values from -6 to 6
- contrast: float32 [2048, 128], P(('hi', 'lo')), may hold values from 0.3 to 3
- coords: bfloat16 [2048, 3, 128], P(('hi', 'lo')), as said below
- neighbours: int32 [2048, 27], P(('hi', 'lo')), may hold values from 0 to 2047, as said below
- partner_perm: int32 [8, 512, 4], P(None, ('hi', 'lo')), may hold values from 0 to 3, each once within a row
- leaf_in: bfloat16 [2048, 64, 128], P(('hi', 'lo')), may hold values from -0.5 to 0.5
- leaf_out: bfloat16 [2048, 64, 128], P(('hi', 'lo')), may hold values from -0.75 to 0.75
- mixing: bfloat16 [8, 2048, 2, 64, 64], P(None, ('hi', 'lo')), may hold values from -0.5 to 0.5
Outputs:
- applied: bfloat16 [2048, 2, 32, 128], P(('hi', 'lo'))
- adjoint_out: bfloat16 [2048, 2, 32, 128], P(('hi', 'lo'))
The draws below stay inside these ranges and needn't reach their ends.
Inputs may be any that keep to these rules, and one draw needn't show every extreme that they name: `neighbours`: the leaf boxes fill a grid of cells whose Morton codes are 0 to 2048 - 1 (bit t of a code is bit t // 3 of the cell's coordinate along component t % 3). Box g owns one cell c(g), and the 4 boxes of device e own the cells with codes e * 4 to e * 4 + 3, in some order. Row g lists, in some order, the boxes of the 27 cells c(g) + o for o in the finite set (-1, 0, 1)^3, each coordinate clamped to the grid. `coords`: the points of box g lie in the unit cube [c(g), c(g) + 1) of its cell; every coordinate is a multiple of 1/8.
All inputs are finite; a program needn't handle non-finite values.
Results may differ from the reference program's by a relative error of at most 0.015.
Values may be sent and summed in bfloat16 or wider, within the bound.
A program may use at most 64 MiB of HBM per device.

```python
import math
import jax
import jax.numpy as jnp
from jax import lax

BOX_DEV = 4
P_SIZE = 128
R = 32
RANK = 64
LEVELS = 8
BOXES = 2048
N_HI = 16
N_LO = 32


def cell_layout(key):
    total_bits = BOXES.bit_length() - 1
    device_total = BOXES // BOX_DEV
    device_keys = jax.random.split(key, device_total)
    orders = jax.vmap(jax.random.permutation, in_axes=(0, None))(device_keys, jnp.arange(BOX_DEV, dtype=jnp.int32))
    cell_of_box = (jnp.arange(device_total, dtype=jnp.int32)[:, None] * BOX_DEV + orders).reshape(-1).astype(jnp.int32)
    box_of_cell = jnp.zeros((BOXES,), jnp.int32).at[cell_of_box].set(jnp.arange(BOXES, dtype=jnp.int32))
    return (total_bits, cell_of_box, box_of_cell)


def decode_cells(cells, total_bits):
    parts = [jnp.zeros_like(cells), jnp.zeros_like(cells), jnp.zeros_like(cells)]
    for bit_index in range(total_bits):
        parts[bit_index % 3] = parts[bit_index % 3] + (cells >> bit_index & 1) * (1 << bit_index // 3)
    return parts


def draw_coords(key, part):
    total_bits, cell_of_box, box_of_cell = cell_layout(key)
    key = jax.random.fold_in(key, 11)
    corner = jnp.stack(decode_cells(cell_of_box, total_bits), axis=1)
    jitter = jax.random.randint(key, (BOXES, 3, P_SIZE), 0, 8)
    return ((corner[:, :, None] * 8 + jitter).astype(jnp.float32) / 8.0).astype(jnp.bfloat16)


def draw_neighbours(key, part):
    total_bits, cell_of_box, box_of_cell = cell_layout(key)
    key = jax.random.fold_in(key, 23)
    parts = decode_cells(cell_of_box, total_bits)
    slots = jnp.arange(27, dtype=jnp.int32)
    shifts = [slots % 3 - 1, slots // 3 % 3 - 1, slots // 9 - 1]
    cells = jnp.zeros((BOXES, 27), jnp.int32)
    for dimension in range(3):
        extent = 1 << len([t for t in range(total_bits) if t % 3 == dimension])
        moved = jnp.clip(parts[dimension][:, None] + shifts[dimension][None, :], 0, extent - 1)
        for bit_index in range(total_bits):
            if bit_index % 3 == dimension:
                cells = cells + (moved >> bit_index // 3 & 1) * (1 << bit_index)
    entries = box_of_cell[cells].astype(jnp.int32)
    row_keys = jax.random.split(key, BOXES)
    shuffled = jax.vmap(jax.random.permutation)(row_keys, entries)
    return shuffled.astype(jnp.int32)


def level_of(key, shape, cuts, smallest, high):
    gain, own = 1.0, jax.random.fold_in(key, 6)
    for position, shards_of in cuts:
        draws = jnp.exp(jax.random.uniform(jax.random.fold_in(own, position), (shards_of,), jnp.float32, smallest / len(cuts), high / len(cuts)))
        gain = gain * jnp.repeat(draws, shape[position] // shards_of).reshape([-1 if axis == position else 1 for axis in range(len(shape))])
    return gain


def scatter_about(stream_key, shape, width, limit, shards=(), kind=jnp.bfloat16):
    drawn = jax.random.normal(stream_key, shape, jnp.float32) * width
    if len(shards) > 0:
        drawn = level_of(stream_key, shape, shards, -0.22, 0.18) * drawn
    return jnp.clip(drawn, min=-limit, max=limit).astype(kind)


def setup_inputs(seed: int = 0) -> dict:
    key_of = jax.random.split(jax.random.key(seed), 10)
    fields = scatter_about(key_of[0], (BOXES, 2, R, P_SIZE), 1.0, 6.0, ((0, 512),))
    adjoint_in = scatter_about(key_of[1], (BOXES, 2, R, P_SIZE), 1.0, 6.0, ((0, 512),))
    contrast = jnp.clip(jnp.exp(math.log(3.0) - 2.3025851 * jax.random.uniform(key_of[2], (BOXES, P_SIZE), jnp.float32) ** level_of(key_of[2], (BOXES, P_SIZE), ((0, 512),), -0.2, 0.2)), 0.3, 3.0)
    coords = draw_coords(jax.random.fold_in(key_of[9], 71), 0)
    neighbours = draw_neighbours(jax.random.fold_in(key_of[9], 71), 0)
    partner_perm = jax.vmap(lambda own: jax.random.permutation(own, BOX_DEV))(jax.random.split(key_of[5], LEVELS * (N_HI * N_LO))).reshape((LEVELS, N_HI * N_LO, BOX_DEV)).astype(jnp.int32)
    leaf_in = scatter_about(key_of[6], (BOXES, RANK, P_SIZE), P_SIZE ** -0.5, 0.5, ((0, 512),))
    leaf_out = scatter_about(key_of[7], (BOXES, RANK, P_SIZE), RANK ** -0.5, 0.75, ((0, 512),))
    mixing = scatter_about(key_of[8], (LEVELS, BOXES, 2, RANK, RANK), (2 * RANK) ** -0.5, 0.5, ((1, 512),))
    return {"fields": fields, "adjoint_in": adjoint_in, "contrast": contrast, "coords": coords, "neighbours": neighbours, "partner_perm": partner_perm, "leaf_in": leaf_in, "leaf_out": leaf_out, "mixing": mixing}


WAVENUMBER = 9.0
SOFTENING = 0.1
HIGH = lax.Precision.HIGHEST

def kernel_block(target, sources):
    spread = target[None, :, :, None].astype(jnp.float32) - sources[:, :, None, :].astype(jnp.float32)
    distance = jnp.sqrt(lax.optimization_barrier(jnp.sum(spread * spread, axis=1)) + SOFTENING * SOFTENING)
    factor = 1.0 / math.sqrt(sources.shape[0] * target.shape[1])
    cosine = factor * jnp.cos(WAVENUMBER * distance) / distance
    sine_part = factor * jnp.sin(WAVENUMBER * distance) / distance
    return jnp.stack([cosine, sine_part], axis=1).astype(jnp.bfloat16)

def near_apply(kernels, sources):
    products = jnp.einsum('kgab,kprb->gpra', kernels.astype(jnp.float32), sources.astype(jnp.float32), precision=HIGH)
    return jnp.stack([products[0, 0] - products[1, 1], products[0, 1] + products[1, 0]])

def near_adjoint(kernels, adjoint_box):
    products = jnp.einsum('kgab,pra->kgprb', kernels.astype(jnp.float32), adjoint_box.astype(jnp.float32), precision=HIGH)
    return jnp.stack([products[:, 0, 0] + products[:, 1, 1], products[:, 0, 1] - products[:, 1, 0]], axis=1)

def mix_forward(coefficient, weight):
    return jnp.einsum('brpk,bmk->brpm', coefficient.astype(jnp.float32), weight.astype(jnp.float32), precision=HIGH)

def mix_backward(coefficient, weight):
    return jnp.einsum('brpm,bmk->brpk', coefficient.astype(jnp.float32), weight.astype(jnp.float32), precision=HIGH)

def reference(fields, adjoint_in, contrast, coords, neighbours, partner_perm, leaf_in, leaf_out, mixing):
    weighted = (contrast[:, None, None, :] * fields.astype(jnp.float32)).astype(jnp.bfloat16)
    block_size = math.gcd(BOXES, 32)

    def visit(accumulated, first_row):
        neighbour_rows = lax.dynamic_slice_in_dim(neighbours, first_row, block_size, 0)
        targets = lax.dynamic_slice_in_dim(coords, first_row, block_size, 0)
        adjoint_rows = lax.dynamic_slice_in_dim(adjoint_in, first_row, block_size, 0)
        kernels = jax.vmap(kernel_block)(targets, coords[neighbour_rows])
        near_field = jax.vmap(near_apply)(kernels, weighted[neighbour_rows])
        spread_terms = jax.vmap(near_adjoint)(kernels, adjoint_rows)
        accumulated = accumulated.at[neighbour_rows.reshape(-1)].add(spread_terms.reshape((-1,) + spread_terms.shape[2:]))
        return (accumulated, near_field)
    starts = jnp.arange(BOXES // block_size, dtype=jnp.int32) * block_size
    near_back, near_field = lax.scan(visit, jnp.zeros((BOXES, 2, R, P_SIZE), jnp.float32), starts)
    near_field = near_field.reshape(BOXES, 2, R, P_SIZE)
    lo_bits = N_LO.bit_length() - 1
    device_ids = jnp.arange(N_HI * N_LO, dtype=jnp.int32)

    def partner_of(level_index):
        flip_bit = level_index if level_index < lo_bits - 1 else level_index + 1
        other_device = jnp.bitwise_xor(device_ids, 1 << flip_bit)
        return (other_device[:, None] * BOX_DEV + partner_perm[level_index]).reshape(-1).astype(jnp.int32)
    coefficient = jnp.einsum('bprx,bkx->brpk', weighted.astype(jnp.float32), leaf_in.astype(jnp.float32), precision=HIGH).astype(jnp.bfloat16)
    for level_index in range(LEVELS):
        partner = partner_of(level_index)
        coefficient = (mix_forward(coefficient, mixing[level_index, :, 0]) + mix_forward(coefficient[partner], mixing[level_index, :, 1])).astype(jnp.bfloat16)
    far_field = jnp.einsum('brpk,bkx->bprx', coefficient.astype(jnp.float32), leaf_out.astype(jnp.float32), precision=HIGH)
    applied = (fields.astype(jnp.float32) - (near_field + far_field)).astype(jnp.bfloat16)
    carried_back = jnp.einsum('bprx,bkx->brpk', adjoint_in.astype(jnp.float32), leaf_out.astype(jnp.float32), precision=HIGH).astype(jnp.bfloat16)
    for level_index in reversed(range(LEVELS)):
        partner = partner_of(level_index)
        carried = mix_backward(carried_back, mixing[level_index, :, 1]).astype(jnp.bfloat16)
        placed = jnp.zeros_like(carried).at[partner].set(carried)
        carried_back = (mix_backward(carried_back, mixing[level_index, :, 0]) + placed.astype(jnp.float32)).astype(jnp.bfloat16)
    far_back = jnp.einsum('brpk,bkx->bprx', carried_back.astype(jnp.float32), leaf_in.astype(jnp.float32), precision=HIGH)
    adjoint_out = (adjoint_in.astype(jnp.float32) - contrast[:, None, None, :] * (near_back + far_back)).astype(jnp.bfloat16)
    return (applied, adjoint_out)
```

```python
import functools
import math

import jax
import jax.numpy as jnp
import numpy as np
from jax import lax
from jax.experimental import pallas as pl
from jax.experimental.pallas import tpu as pltpu
from jax.sharding import PartitionSpec as P

WAVENUMBER = 9.0
SOFTENING = 0.1
MESH = pl.DeviceIdType.MESH
ROWS = 144
MAGIC = 12582912.0
BF = jnp.bfloat16
F32 = jnp.float32
NT = (((1,), (1,)), ((), ()))
TN = (((0,), (0,)), ((), ()))


def fit(function, degree):
    nodes = 0.125 * (1.0 - np.cos(np.pi * (np.arange(400) + 0.5) / 400))
    poly = np.polynomial.chebyshev.Chebyshev.fit(nodes, function(nodes), degree, domain=[0, 0.25])
    return [float(c) for c in poly.convert(kind=np.polynomial.Polynomial).coef]


CYCLES = WAVENUMBER / (2 * math.pi)
COS_POLY = fit(lambda s: np.cos(2 * np.pi * np.sqrt(s)), 4)
SIN_POLY = fit(lambda s: np.sin(2 * np.pi * np.sqrt(s)) / np.sqrt(s), 3)


def horner(coefs, s):
    value = coefs[-1] * s + coefs[-2]
    for c in coefs[-3::-1]:
        value = value * s + c
    return value


def oscillation(squared, scale):
    w = squared * (CYCLES * CYCLES / 64.0) + CYCLES * CYCLES * SOFTENING * SOFTENING
    r = lax.rsqrt(w)
    y = w * r
    f = y - ((y + MAGIC) - MAGIC)
    s = f * f
    amp = scale * CYCLES
    real = horner([amp * c for c in COS_POLY], s) * r
    imag = horner([amp * c for c in SIN_POLY], s) * (f * r)
    return real.astype(BF), imag.astype(BF)


def spread(value, bits):
    total = 0
    for place, bit in enumerate(bits):
        total = total + (value // (1 << place)) % 2 * (1 << bit)
    return total


def dot(a, b, dims=None):
    if dims is None:
        return jnp.dot(a, b, preferred_element_type=F32)
    return lax.dot_general(a, b, dims, preferred_element_type=F32)


def kernel(
    n_hi, n_lo, scale,
    cell_ref, perm_ref, fields_ref, adj_ref, contrast_ref, coords_ref, lin_ref, lout_ref, mix_ref,
    out_ref, adj_out_ref,
    grid, tgt, acc, wbuf, ll_in, ll_out, blocks, fsend, bsend, brecv, carry,
    send_sem, recv_sem, *frecv,
):
    e = lax.axis_index("hi") * n_lo + lax.axis_index("lo")
    bits = (n_hi * n_lo).bit_length() - 1
    lo_bits = n_lo.bit_length() - 1
    levels = [b for b in range(bits) if b != lo_bits - 1]
    depth = len(levels)
    boxes = 4

    def where_is(device):
        return (device // n_lo, device % n_lo)

    def flip(bit):
        return e + (1 - 2 * ((e // (1 << bit)) % 2)) * (1 << bit)

    dims = []
    for d in range(3):
        own_bits = [t - 2 for t in range(2, bits + 2) if t % 3 == d]
        coord = 0
        for place, bit in enumerate(own_bits):
            coord = coord + (e // (1 << bit)) % 2 * (1 << place)
        rest = e - spread(coord, own_bits)
        dims.append((own_bits, coord, rest, 1 << len(own_bits)))

    def at(d, coordinate):
        own_bits, _, rest, _ = dims[d]
        return rest + spread(coordinate, own_bits)

    (_, xc, _, nx), (_, yc, _, ny), (_, zc, _, nz) = dims
    par = zc % 2
    mate = 2 - 2 * par
    third = 2 * par
    z_to = zc + 2 - 4 * par
    z_from = zc - 2 + 4 * par
    z_sends = jnp.logical_and(z_to >= 0, z_to < nz)
    z_receives = jnp.logical_and(z_from >= 0, z_from < nz)

    barrier = pltpu.get_barrier_semaphore()

    def greet(device):
        pl.semaphore_signal(barrier, inc=1, device_id=where_is(device), device_id_type=MESH)

    for bit in levels:
        greet(flip(bit))
    others = []
    for d, n, c in ((0, nx, xc), (1, ny, yc)):
        others.append((c > 0, at(d, (c + n - 1) % n)))
        others.append((c < n - 1, at(d, (c + 1) % n)))
    others.append((z_sends, at(2, (z_to + nz) % nz)))
    others.append((z_receives, at(2, (z_from + nz) % nz)))
    for there, device in others:
        @pl.when(there)
        def _(device=device):
            greet(device)

    box_of = []
    rasters = [(cell_ref[j, 1] % 2) * 2 + cell_ref[j, 0] % 2 for j in range(boxes)]
    for s in range(boxes):
        found = 0
        for j in range(1, boxes):
            found = found + jnp.where(rasters[j] == s, j, 0)
        box_of.append(jnp.minimum(found, boxes - 1))

    rank = lin_ref.shape[1]
    for g in range(boxes):
        for ll, leaf in ((ll_in, lin_ref), (ll_out, lout_ref)):
            zero = jnp.zeros((rank, 128), BF)
            ll[g, 0:rank, 0:128] = leaf[g]
            ll[g, 0:rank, 128:256] = zero
            ll[g, rank : 2 * rank, 0:128] = zero
            ll[g, rank : 2 * rank, 128:256] = leaf[g]
        wbuf[g] = (contrast_ref[g : g + 1, :] * fields_ref[g].astype(F32)).astype(BF)
        w = wbuf[g]
        lhs = jnp.concatenate([w[0:32], w[32:64]], axis=1)
        fsend[0, g] = dot(lhs, ll_in[g], NT).astype(BF)

    row = lax.broadcasted_iota(jnp.int32, (16, 128), 0)
    for s in range(boxes):
        b = box_of[s]
        place = (1, 1 + s // 2, 1 + s % 2)
        grid[place + (slice(0, 64),)] = wbuf[b]
        grid[place + (slice(64, 128),)] = adj_ref[b]
        c = coords_ref[b].astype(F32) * 8.0
        cx, cy, cz = c[0:1], c[1:2], c[2:3]
        norm = cx * cx + cy * cy + cz * cz
        high = jnp.floor(norm * (1.0 / 256.0)) * 256.0
        low = norm - high
        one = jnp.ones_like(low)
        zero = jnp.zeros_like(low)

        def stack(rows):
            value = jnp.broadcast_to(zero, (16, 128))
            for k, r in enumerate(rows):
                value = jnp.where(row == k, r, value)
            return value.astype(BF)

        grid[place + (slice(128, 144),)] = stack([cx, cy, cz, high, low, one, one])
        tgt[s] = stack([-2.0 * cx, -2.0 * cy, -2.0 * cz, one, one, high, low])

    def build(i, _):
        l, g = i // boxes, i % boxes
        zero = jnp.zeros((rank, rank), BF)
        for part in range(2):
            m = mix_ref[l, g, part]
            base = part * 128
            blocks[l, g, 0:rank, base : base + 128] = jnp.concatenate([m, zero], axis=1)
            blocks[l, g, rank : 2 * rank, base : base + 128] = jnp.concatenate([zero, m], axis=1)
        return 0

    lax.fori_loop(0, depth * boxes, build, 0)

    def inverse(l, s):
        found = 0
        for j in range(1, boxes):
            found = found + jnp.where(perm_ref[l, j] == s, j, 0)
        return jnp.minimum(found, boxes - 1)

    def back_products(l, backs):
        own = []
        for g in range(boxes):
            both = dot(backs[g], blocks[l, g])
            own.append(both[:, 0:128])
            carry[l, g] = both[:, 128:256].astype(BF)
        for s in range(boxes):
            bsend[l, s] = carry[l, inverse(l, s)]
        return own

    backs = []
    for g in range(boxes):
        a = adj_ref[g]
        lhs = jnp.concatenate([a[0:32], a[32:64]], axis=1)
        backs.append(dot(lhs, ll_out[g], NT).astype(BF))
    own_terms = back_products(depth - 1, backs)
    acc[...] = jnp.zeros_like(acc)

    def remote(src, dst, sem, device):
        return pltpu.make_async_remote_copy(
            src_ref=src, dst_ref=dst, send_sem=send_sem.at[sem], recv_sem=recv_sem.at[sem],
            device_id=where_is(device), device_id_type=MESH,
        )

    def forward_copy(l):
        return remote(fsend.at[l], frecv[l], l, flip(levels[l]))

    def back_copy(l):
        return remote(bsend.at[l], brecv.at[l], depth + l, flip(levels[l]))

    first_sem = 2 * depth
    z1 = remote(
        grid.at[1, pl.ds(1, 2), pl.ds(1, 2)],
        grid.at[third, pl.ds(1, 2), pl.ds(1, 2)],
        first_sem, flip(0),
    )
    z2 = remote(
        grid.at[mate, pl.ds(1, 2), pl.ds(1, 2)],
        grid.at[third, pl.ds(1, 2), pl.ds(1, 2)],
        first_sem + 1, at(2, (z_to + nz) % nz),
    )

    def y_copies(plane, kind):
        sem = first_sem + 2 + 4 * kind
        up = remote(
            grid.at[plane, 2, pl.ds(1, 2)], grid.at[plane, 0, pl.ds(1, 2)],
            sem, at(1, (yc + 1) % ny),
        )
        down = remote(
            grid.at[plane, 1, pl.ds(1, 2)], grid.at[plane, 3, pl.ds(1, 2)],
            sem + 1, at(1, (yc + ny - 1) % ny),
        )
        return ((up, yc < ny - 1, yc > 0), (down, yc > 0, yc < ny - 1))

    def x_copies(plane, kind):
        sem = first_sem + 4 + 4 * kind
        up = remote(
            grid.at[plane, pl.ds(0, 4), 2], grid.at[plane, pl.ds(0, 4), 0],
            sem, at(0, (xc + 1) % nx),
        )
        down = remote(
            grid.at[plane, pl.ds(0, 4), 1], grid.at[plane, pl.ds(0, 4), 3],
            sem + 1, at(0, (xc + nx - 1) % nx),
        )
        return ((up, xc < nx - 1, xc > 0), (down, xc > 0, xc < nx - 1))

    def start(copies):
        for copy, sends, _ in copies:
            @pl.when(sends)
            def _(copy=copy):
                copy.start()

    def arrive(copies):
        for copy, _, receives in copies:
            @pl.when(receives)
            def _(copy=copy):
                copy.wait_recv()

    def sent(copies):
        for copy, sends, _ in copies:
            @pl.when(sends)
            def _(copy=copy):
                copy.wait_send()

    own_y, own_x = y_copies(1, 0), x_copies(1, 0)
    mate_y, mate_x = y_copies(mate, 1), x_copies(mate, 1)
    third_y, third_x = y_copies(third, 2), x_copies(third, 2)
    z2_copies = ((z2, z_sends, z_receives),)

    y_low, y_high = 1 - (yc + ny - 1) // ny, (yc + 1) // ny
    x_low, x_high = 1 - (xc + nx - 1) // nx, (xc + 1) // nx

    def clamp(v, low, high):
        return v + (1 - (v + 3) // 4) * low - (v // 3) * high

    def near(plane, first, last):
        def step(i, _):
            t, dy = i // 3, i % 3
            ty, tx = t // 2, t % 2
            y = clamp(ty + dy, y_low, y_high)
            goal = tgt[t]
            values, reals, imags = [], [], []
            for dx in range(3):
                x = clamp(tx + dx, x_low, x_high)
                values.append(grid[plane, y, x, 0:128])
                squared = dot(grid[plane, y, x, 128:144], goal, TN)
                real, imag = oscillation(squared, scale)
                reals.append(real)
                imags.append(imag)
            rhs = jnp.concatenate(
                [jnp.concatenate(reals, axis=0), jnp.concatenate(imags, axis=0)], axis=1
            )
            acc[t] = acc[t] + dot(jnp.concatenate(values, axis=1), rhs)
            return 0

        lax.fori_loop(first * 3, last * 3, step, 0)

    peers = depth
    for there, _ in others:
        peers = peers + there.astype(jnp.int32)
    pl.semaphore_wait(barrier, peers)

    forward_copy(0).start()
    back_copy(depth - 1).start()
    z1.start()
    start(own_y)

    coefs = [fsend[0, g] for g in range(boxes)]

    def step(i, coefs, own_terms):
        mine = [dot(coefs[g], blocks[i, g, :, 0:128], NT) for g in range(boxes)]
        forward_copy(i).wait_recv()
        new = []
        for g in range(boxes):
            arrived = frecv[i][perm_ref[i, g]]
            c = (mine[g] + dot(arrived, blocks[i, g, :, 128:256], NT)).astype(BF)
            new.append(c)
            if i + 1 < depth:
                fsend[i + 1, g] = c
        if i + 1 < depth:
            forward_copy(i + 1).start()
        l = depth - 1 - i
        back_copy(l).wait_recv()
        backs = [(own_terms[g] + brecv[l, g].astype(F32)).astype(BF) for g in range(boxes)]
        if l > 0:
            own_terms = back_products(l - 1, backs)
            back_copy(l - 1).start()
        return new, backs, own_terms

    def after(i):
        if i == 0:
            arrive(own_y)
            start(own_x)
        if i == 1:
            arrive(own_x)
            near(1, 0, 1)
        if i == 2:
            near(1, 1, 2)
        if i == 3:
            near(1, 2, 3)
        if i == 4:
            z1.wait_recv()
            start(z2_copies)
            start(mate_y)
            near(1, 3, 4)
        if i == 5:
            arrive(z2_copies)
            arrive(mate_y)

            @pl.when(z_receives)
            def _():
                start(third_y)

            start(mate_x)
        if i == 6:
            @pl.when(z_receives)
            def _():
                arrive(third_y)
                start(third_x)

            arrive(mate_x)
            near(mate, 0, 2)

    for i in range(depth):
        coefs, backs, own_terms = step(i, coefs, own_terms)
        after(i)
    for i in range(depth, 8):
        after(i)
    near(mate, 2, 4)

    @pl.when(z_receives)
    def _():
        arrive(third_x)

    near(third + (1 - third) * (1 - z_receives.astype(jnp.int32)), 0, 4)

    for g in range(boxes):
        a = acc[rasters[g]]
        ar, ai = a[:, 0:128], a[:, 128:256]
        far = dot(coefs[g], ll_out[g])
        out_ref[g, 0:32] = (
            fields_ref[g, 0:32].astype(F32) - (ar[0:32] - ai[32:64] + far[:, 0:128])
        ).astype(BF)
        out_ref[g, 32:64] = (
            fields_ref[g, 32:64].astype(F32) - (ai[0:32] + ar[32:64] + far[:, 128:256])
        ).astype(BF)
        far = dot(backs[g], ll_in[g])
        contrast = contrast_ref[g : g + 1, :]
        adj_out_ref[g, 0:32] = (
            adj_ref[g, 0:32].astype(F32) - contrast * (ar[64:96] + ai[96:128] + far[:, 0:128])
        ).astype(BF)
        adj_out_ref[g, 32:64] = (
            adj_ref[g, 32:64].astype(F32) - contrast * (ar[96:128] - ai[64:96] + far[:, 128:256])
        ).astype(BF)

    for l in range(depth):
        forward_copy(l).wait_send()
        back_copy(l).wait_send()
    z1.wait_send()
    sent(z2_copies)
    sent(own_y)
    sent(own_x)
    sent(mate_y)
    sent(mate_x)

    @pl.when(z_receives)
    def _():
        sent(third_y)
        sent(third_x)


def body(fields, adjoint_in, contrast, coords, neighbours, partner_perm, leaf_in, leaf_out, mixing):
    boxes, parts, sides, points = fields.shape
    depth = mixing.shape[0]
    rank = leaf_in.shape[1]
    n_hi, n_lo = lax.axis_size("hi"), lax.axis_size("lo")
    cells = jnp.floor(coords[:, 0:2, 0].astype(F32)).astype(jnp.int32)
    scale = 1.0 / math.sqrt(27 * points)
    vmem = pl.BlockSpec(memory_space=pltpu.VMEM)
    smem = pl.BlockSpec(memory_space=pltpu.SMEM)
    flat = (boxes, parts * sides, points)
    copies = 2 * depth + 14
    level = (depth, boxes, sides, 2 * rank)
    out = pl.pallas_call(
        functools.partial(kernel, n_hi, n_lo, scale),
        out_shape=[jax.ShapeDtypeStruct(flat, BF)] * 2,
        in_specs=[smem] * 2 + [vmem] * 7,
        out_specs=[vmem] * 2,
        scratch_shapes=[
            pltpu.VMEM((3, 4, 4, ROWS, points), BF),
            pltpu.VMEM((boxes, 16, points), BF),
            pltpu.VMEM((boxes, 4 * sides, 2 * points), F32),
            pltpu.VMEM(flat, BF),
            pltpu.VMEM((boxes, 2 * rank, 2 * points), BF),
            pltpu.VMEM((boxes, 2 * rank, 2 * points), BF),
            pltpu.VMEM((depth, boxes, 2 * rank, 4 * rank), BF),
            pltpu.VMEM(level, BF),
            pltpu.VMEM(level, BF),
            pltpu.VMEM(level, BF),
            pltpu.VMEM(level, BF),
            pltpu.SemaphoreType.DMA((copies,)),
            pltpu.SemaphoreType.DMA((copies,)),
        ]
        + [pltpu.VMEM(level[1:], BF)] * depth,
        compiler_params=pltpu.CompilerParams(
            collective_id=0, has_side_effects=True, vmem_limit_bytes=40 * 1024 * 1024
        ),
        name="operator",
    )(
        cells,
        partner_perm.reshape(depth, boxes),
        fields.reshape(flat),
        adjoint_in.reshape(flat),
        contrast,
        coords,
        leaf_in,
        leaf_out,
        mixing,
    )
    return (out[0].reshape(fields.shape), out[1].reshape(fields.shape))


def solution(mesh):
    split = ("hi", "lo")
    in_specs = (
        P(split, None, None, None),
        P(split, None, None, None),
        P(split, None),
        P(split, None, None),
        P(split, None),
        P(None, split, None),
        P(split, None, None),
        P(split, None, None),
        P(None, split, None, None, None),
    )
    out_specs = (P(split, None, None, None), P(split, None, None, None))
    return jax.shard_map(body, mesh=mesh, in_specs=in_specs, out_specs=out_specs, check_vma=False)
```

```python
import functools
import math

import jax
import jax.numpy as jnp
import numpy as np
from jax import lax
from jax.experimental import pallas as pl
from jax.experimental.pallas import tpu as pltpu
from jax.sharding import PartitionSpec as P

WAVENUMBER = 9.0
SOFTENING = 0.1
MESH = pl.DeviceIdType.MESH
ROWS = 144
MAGIC = 12582912.0
BF = jnp.bfloat16
F32 = jnp.float32
NT = (((1,), (1,)), ((), ()))
TN = (((0,), (0,)), ((), ()))


def fit(function, degree):
    nodes = 0.125 * (1.0 - np.cos(np.pi * (np.arange(400) + 0.5) / 400))
    poly = np.polynomial.chebyshev.Chebyshev.fit(nodes, function(nodes), degree, domain=[0, 0.25])
    return [float(c) for c in poly.convert(kind=np.polynomial.Polynomial).coef]


CYCLES = WAVENUMBER / (2 * math.pi)
COS_POLY = fit(lambda s: np.cos(2 * np.pi * np.sqrt(s)), 4)
SIN_POLY = fit(lambda s: np.sin(2 * np.pi * np.sqrt(s)) / np.sqrt(s), 3)


def horner(coefs, s):
    value = coefs[-1] * s + coefs[-2]
    for c in coefs[-3::-1]:
        value = value * s + c
    return value


def oscillation(squared, scale):
    w = squared * (CYCLES * CYCLES / 64.0) + CYCLES * CYCLES * SOFTENING * SOFTENING
    r = lax.rsqrt(w)
    y = w * r
    f = y - ((y + MAGIC) - MAGIC)
    s = f * f
    amp = scale * CYCLES
    real = horner([amp * c for c in COS_POLY], s) * r
    imag = horner([amp * c for c in SIN_POLY], s) * (f * r)
    return real.astype(BF), imag.astype(BF)


def spread(value, bits):
    total = 0
    for place, bit in enumerate(bits):
        total = total + (value // (1 << place)) % 2 * (1 << bit)
    return total


def dot(a, b, dims=None):
    if dims is None:
        return jnp.dot(a, b, preferred_element_type=F32)
    return lax.dot_general(a, b, dims, preferred_element_type=F32)


def kernel(
    n_hi, n_lo, scale,
    perm_ref, coords_ref, *refs,
):
    operands, refs = refs[:6], refs[6:]
    out_ref, adj_out_ref, *refs = refs
    (fields_ref, adj_ref, contrast_ref, lin_ref, lout_ref, mix_ref), refs = refs[:6], refs[6:]
    (
        grid, tgt, acc, ll_in, ll_out, blocks, fsend, bsend, brecv, carry, relays,
        send_sem, recv_sem, load_sem, *frecv,
    ) = refs
    loads = [
        pltpu.make_async_copy(src, dst, load_sem.at[i])
        for i, (src, dst) in enumerate(
            zip(operands, (fields_ref, adj_ref, contrast_ref, lin_ref, lout_ref, mix_ref))
        )
    ]
    for load in loads:
        load.start()
    e = lax.axis_index("hi") * n_lo + lax.axis_index("lo")
    bits = (n_hi * n_lo).bit_length() - 1
    lo_bits = n_lo.bit_length() - 1
    levels = [b for b in range(bits) if b != lo_bits - 1]
    depth = len(levels)
    boxes = 4

    def where_is(device):
        return (device // n_lo, device % n_lo)

    def flip(bit):
        return e + (1 - 2 * ((e // (1 << bit)) % 2)) * (1 << bit)

    dims = []
    for d in range(3):
        own_bits = [t - 2 for t in range(2, bits + 2) if t % 3 == d]
        coord = 0
        for place, bit in enumerate(own_bits):
            coord = coord + (e // (1 << bit)) % 2 * (1 << place)
        rest = e - spread(coord, own_bits)
        dims.append((own_bits, coord, rest, 1 << len(own_bits)))

    def at(d, coordinate):
        own_bits, _, rest, _ = dims[d]
        return rest + spread(coordinate, own_bits)

    (_, xc, _, nx), (_, yc, _, ny), (_, zc, _, nz) = dims
    par = zc % 2
    mate = 2 - 2 * par
    third = 2 * par
    z_to = zc + 2 - 4 * par
    z_from = zc - 2 + 4 * par
    z_sends = jnp.logical_and(z_to >= 0, z_to < nz)
    z_receives = jnp.logical_and(z_from >= 0, z_from < nz)

    ring_bits = list(range(lo_bits + 1, bits)) + [0]
    ring = 1 << len(ring_bits)
    zpos = 0
    for place, bit in enumerate(ring_bits):
        zpos = zpos + (e // (1 << bit)) % 2 * (1 << place)

    def on_ring(shift):
        return e - spread(zpos, ring_bits) + spread((zpos + ring + shift) % ring, ring_bits)

    def side(shift):
        return (zpos + ring + shift) % ring // (ring // 2)

    far_hop = ring // 2 - 1

    barrier = pltpu.get_barrier_semaphore()

    def greet(device):
        pl.semaphore_signal(barrier, inc=1, device_id=where_is(device), device_id_type=MESH)

    for bit in levels:
        greet(flip(bit))
    for shift in (far_hop, -far_hop, 1, -1):
        greet(on_ring(shift))
    others = []
    for d, n, c in ((0, nx, xc), (1, ny, yc)):
        others.append((c > 0, at(d, (c + n - 1) % n)))
        others.append((c < n - 1, at(d, (c + 1) % n)))
    others.append((z_sends, at(2, (z_to + nz) % nz)))
    others.append((z_receives, at(2, (z_from + nz) % nz)))
    for there, device in others:
        @pl.when(there)
        def _(device=device):
            greet(device)

    rank = lin_ref.shape[1]
    c = coords_ref[...].astype(F32)
    cells = jnp.floor(c)
    odd = cells - 2.0 * jnp.floor(0.5 * cells)
    raster = odd[0] + 2.0 * odd[1]
    c = c * 8.0
    norm = c[0] * c[0] + c[1] * c[1] + c[2] * c[2]
    high = jnp.floor(norm * (1.0 / 256.0)) * 256.0
    low = norm - high

    def holds(g, s):
        return raster[g : g + 1] == float(s)

    def pick(s, values):
        total = values[0]
        for g in range(1, boxes):
            total = jnp.where(holds(g, s), values[g], total)
        return total

    row = lax.broadcasted_iota(jnp.int32, (16, 128), 0)

    def stack(rows):
        value = jnp.zeros((16, 128), F32)
        for k, r in enumerate(rows):
            value = jnp.where(row == k, r, value)
        return value.astype(BF)

    one = jnp.ones((1, 128), F32)
    for s in range(boxes):
        x, y, z, h, w = (
            pick(s, [v[g : g + 1] for g in range(boxes)]) for v in (c[0], c[1], c[2], high, low)
        )
        grid[1, 1 + s // 2, 1 + s % 2, 128:144] = stack([x, y, z, h, w, one, one])
        tgt[s] = stack([-2.0 * x, -2.0 * y, -2.0 * z, one, one, h, w])

    for load in loads[:5]:
        load.wait()
    weighted = []
    for g in range(boxes):
        for ll, leaf in ((ll_in, lin_ref), (ll_out, lout_ref)):
            zero = jnp.zeros((rank, 128), BF)
            ll[g, 0:rank, 0:128] = leaf[g]
            ll[g, 0:rank, 128:256] = zero
            ll[g, rank : 2 * rank, 0:128] = zero
            ll[g, rank : 2 * rank, 128:256] = leaf[g]
        w = contrast_ref[g : g + 1, :] * fields_ref[g].astype(F32)
        weighted.append(w)
        lhs = jnp.concatenate([w[0:32], w[32:64]], axis=1).astype(BF)
        fsend[0, g] = dot(lhs, ll_in[g], NT).astype(BF)
    for s in range(boxes):
        place = (1, 1 + s // 2, 1 + s % 2)
        grid[place + (slice(0, 64),)] = pick(s, weighted).astype(BF)
        grid[place + (slice(64, 128),)] = pick(
            s, [adj_ref[g].astype(F32) for g in range(boxes)]
        ).astype(BF)

    loads[5].wait()

    def build(i, _):
        l, g = i // boxes, i % boxes
        zero = jnp.zeros((rank, rank), BF)
        for part in range(2):
            m = mix_ref[l, g, part]
            base = part * 128
            blocks[l, g, 0:rank, base : base + 128] = jnp.concatenate([m, zero], axis=1)
            blocks[l, g, rank : 2 * rank, base : base + 128] = jnp.concatenate([zero, m], axis=1)
        return 0

    lax.fori_loop(0, depth * boxes, build, 0)

    def inverse(l, s):
        found = 0
        for j in range(1, boxes):
            found = found + jnp.where(perm_ref[j, l] == s, j, 0)
        return jnp.minimum(found, boxes - 1)

    def back_products(l, backs):
        own = []
        for g in range(boxes):
            both = dot(backs[g], blocks[l, g])
            own.append(both[:, 0:128])
            carry[l, g] = both[:, 128:256].astype(BF)
        for s in range(boxes):
            bsend[l, s] = carry[l, inverse(l, s)]
        return own

    backs = []
    for g in range(boxes):
        a = adj_ref[g]
        lhs = jnp.concatenate([a[0:32], a[32:64]], axis=1)
        backs.append(dot(lhs, ll_out[g], NT).astype(BF))
    own_terms = back_products(depth - 1, backs)
    acc[...] = jnp.zeros_like(acc)

    def remote(src, dst, sem, device):
        return pltpu.make_async_remote_copy(
            src_ref=src, dst_ref=dst, send_sem=send_sem.at[sem], recv_sem=recv_sem.at[sem],
            device_id=where_is(device), device_id_type=MESH,
        )

    def forward_copy(l):
        return remote(fsend.at[l], frecv[l], l, flip(levels[l]))

    def back_copy(l):
        return remote(bsend.at[l], brecv.at[l], depth + l, flip(levels[l]))

    first_sem = 2 * depth
    last_sem = first_sem + 14
    up_first = remote(
        grid.at[1, 1, pl.ds(1, 2)], relays.at[0], first_sem, on_ring(far_hop)
    )
    down_first = remote(
        grid.at[1, 2, pl.ds(1, 2)], relays.at[1], last_sem, on_ring(-far_hop)
    )
    up_last = remote(
        relays.at[0], grid.at[2 * side(-far_hop), 1, pl.ds(1, 2)], last_sem + 1, on_ring(1)
    )
    down_last = remote(
        relays.at[1], grid.at[2 * side(far_hop), 2, pl.ds(1, 2)], last_sem + 2, on_ring(-1)
    )
    z2 = remote(
        grid.at[mate, pl.ds(1, 2), pl.ds(1, 2)],
        grid.at[third, pl.ds(1, 2), pl.ds(1, 2)],
        first_sem + 1, at(2, (z_to + nz) % nz),
    )

    def y_copies(plane, kind):
        sem = first_sem + 2 + 4 * kind
        up = remote(
            grid.at[plane, 2, pl.ds(1, 2)], grid.at[plane, 0, pl.ds(1, 2)],
            sem, at(1, (yc + 1) % ny),
        )
        down = remote(
            grid.at[plane, 1, pl.ds(1, 2)], grid.at[plane, 3, pl.ds(1, 2)],
            sem + 1, at(1, (yc + ny - 1) % ny),
        )
        return ((up, yc < ny - 1, yc > 0), (down, yc > 0, yc < ny - 1))

    def x_copies(plane, kind):
        sem = first_sem + 4 + 4 * kind
        up = remote(
            grid.at[plane, pl.ds(0, 4), 2], grid.at[plane, pl.ds(0, 4), 0],
            sem, at(0, (xc + 1) % nx),
        )
        down = remote(
            grid.at[plane, pl.ds(0, 4), 1], grid.at[plane, pl.ds(0, 4), 3],
            sem + 1, at(0, (xc + nx - 1) % nx),
        )
        return ((up, xc < nx - 1, xc > 0), (down, xc > 0, xc < nx - 1))

    def start(copies):
        for copy, sends, _ in copies:
            @pl.when(sends)
            def _(copy=copy):
                copy.start()

    def arrive(copies):
        for copy, _, receives in copies:
            @pl.when(receives)
            def _(copy=copy):
                copy.wait_recv()

    def sent(copies):
        for copy, sends, _ in copies:
            @pl.when(sends)
            def _(copy=copy):
                copy.wait_send()

    own_y, own_x = y_copies(1, 0), x_copies(1, 0)
    mate_y, mate_x = y_copies(mate, 1), x_copies(mate, 1)
    third_y, third_x = y_copies(third, 2), x_copies(third, 2)
    z2_copies = ((z2, z_sends, z_receives),)

    y_low, y_high = 1 - (yc + ny - 1) // ny, (yc + 1) // ny
    x_low, x_high = 1 - (xc + nx - 1) // nx, (xc + 1) // nx

    def clamp(v, low, high):
        return v + (1 - (v + 3) // 4) * low - (v // 3) * high

    def near(plane, first, last):
        def step(i, _):
            t, dy = i // 3, i % 3
            ty, tx = t // 2, t % 2
            y = clamp(ty + dy, y_low, y_high)
            goal = tgt[t]
            values, reals, imags = [], [], []
            for dx in range(3):
                x = clamp(tx + dx, x_low, x_high)
                values.append(grid[plane, y, x, 0:128])
                squared = dot(grid[plane, y, x, 128:144], goal, TN)
                real, imag = oscillation(squared, scale)
                reals.append(real)
                imags.append(imag)
            rhs = jnp.concatenate(
                [jnp.concatenate(reals, axis=0), jnp.concatenate(imags, axis=0)], axis=1
            )
            acc[t] = acc[t] + dot(jnp.concatenate(values, axis=1), rhs)
            return 0

        lax.fori_loop(first * 3, last * 3, step, 0)

    peers = depth + 4
    for there, _ in others:
        peers = peers + there.astype(jnp.int32)
    pl.semaphore_wait(barrier, peers)

    forward_copy(0).start()
    back_copy(depth - 1).start()
    up_first.start()
    down_first.start()
    start(own_y)

    coefs = [fsend[0, g] for g in range(boxes)]

    def step(i, coefs, own_terms):
        mine = [dot(coefs[g], blocks[i, g, :, 0:128], NT) for g in range(boxes)]
        forward_copy(i).wait_recv()
        new = []
        for g in range(boxes):
            arrived = frecv[i][perm_ref[g, i]]
            c = (mine[g] + dot(arrived, blocks[i, g, :, 128:256], NT)).astype(BF)
            new.append(c)
            if i + 1 < depth:
                fsend[i + 1, g] = c
        if i + 1 < depth:
            forward_copy(i + 1).start()
        l = depth - 1 - i
        back_copy(l).wait_recv()
        backs = [(own_terms[g] + brecv[l, g].astype(F32)).astype(BF) for g in range(boxes)]
        if l > 0:
            own_terms = back_products(l - 1, backs)
            back_copy(l - 1).start()
        return new, backs, own_terms

    def after(i):
        if i == 0:
            arrive(own_y)
            start(own_x)
        if i == 1:
            up_first.wait_recv()
            up_last.start()
            down_first.wait_recv()
            down_last.start()
        if i == 2:
            arrive(own_x)
            near(1, 0, 1)
            up_last.wait_recv()
            down_last.wait_recv()
            start(z2_copies)
            start(mate_y)
        if i == 3:
            near(1, 1, 2)
            arrive(mate_y)
            start(mate_x)
            arrive(z2_copies)

            @pl.when(z_receives)
            def _():
                start(third_y)
        if i == 4:
            near(1, 2, 3)

            @pl.when(z_receives)
            def _():
                arrive(third_y)
                start(third_x)
        if i == 5:
            near(1, 3, 4)
        if i == 6:
            arrive(mate_x)
            near(mate, 0, 2)

    for i in range(depth):
        coefs, backs, own_terms = step(i, coefs, own_terms)
        after(i)
    for i in range(depth, 8):
        after(i)
    near(mate, 2, 4)

    @pl.when(z_receives)
    def _():
        arrive(third_x)

    near(third + (1 - third) * (1 - z_receives.astype(jnp.int32)), 0, 4)

    for g in range(boxes):
        a = acc[0]
        for s in range(1, boxes):
            inside = jnp.concatenate([holds(g, s), holds(g, s)], axis=1)
            a = jnp.where(inside, acc[s], a)
        ar, ai = a[:, 0:128], a[:, 128:256]
        far = dot(coefs[g], ll_out[g])
        out_ref[g, 0:32] = (
            fields_ref[g, 0:32].astype(F32) - (ar[0:32] - ai[32:64] + far[:, 0:128])
        ).astype(BF)
        out_ref[g, 32:64] = (
            fields_ref[g, 32:64].astype(F32) - (ai[0:32] + ar[32:64] + far[:, 128:256])
        ).astype(BF)
        far = dot(backs[g], ll_in[g])
        contrast = contrast_ref[g : g + 1, :]
        adj_out_ref[g, 0:32] = (
            adj_ref[g, 0:32].astype(F32) - contrast * (ar[64:96] + ai[96:128] + far[:, 0:128])
        ).astype(BF)
        adj_out_ref[g, 32:64] = (
            adj_ref[g, 32:64].astype(F32) - contrast * (ar[96:128] - ai[64:96] + far[:, 128:256])
        ).astype(BF)

    for l in range(depth):
        forward_copy(l).wait_send()
        back_copy(l).wait_send()
    up_first.wait_send()
    down_first.wait_send()
    up_last.wait_send()
    down_last.wait_send()
    sent(z2_copies)
    sent(own_y)
    sent(own_x)
    sent(mate_y)
    sent(mate_x)

    @pl.when(z_receives)
    def _():
        sent(third_y)
        sent(third_x)


def body(fields, adjoint_in, contrast, coords, neighbours, partner_perm, leaf_in, leaf_out, mixing):
    boxes, parts, sides, points = fields.shape
    depth = mixing.shape[0]
    rank = leaf_in.shape[1]
    n_hi, n_lo = lax.axis_size("hi"), lax.axis_size("lo")
    scale = 1.0 / math.sqrt(27 * points)
    vmem = pl.BlockSpec(memory_space=pltpu.VMEM)
    smem = pl.BlockSpec(memory_space=pltpu.SMEM)
    away = pl.BlockSpec(memory_space=pl.ANY)
    flat = (boxes, parts * sides, points)
    copies = 2 * depth + 17
    level = (depth, boxes, sides, 2 * rank)
    inputs = (
        fields.reshape(flat), adjoint_in.reshape(flat), contrast, leaf_in, leaf_out, mixing,
    )
    out = pl.pallas_call(
        functools.partial(kernel, n_hi, n_lo, scale),
        out_shape=[jax.ShapeDtypeStruct(flat, BF)] * 2,
        in_specs=[smem, vmem] + [away] * 6,
        out_specs=[vmem] * 2,
        scratch_shapes=[pltpu.VMEM(v.shape, v.dtype) for v in inputs]
        + [
            pltpu.VMEM((3, 4, 4, ROWS, points), BF),
            pltpu.VMEM((boxes, 16, points), BF),
            pltpu.VMEM((boxes, 4 * sides, 2 * points), F32),
            pltpu.VMEM((boxes, 2 * rank, 2 * points), BF),
            pltpu.VMEM((boxes, 2 * rank, 2 * points), BF),
            pltpu.VMEM((depth, boxes, 2 * rank, 4 * rank), BF),
            pltpu.VMEM(level, BF),
            pltpu.VMEM(level, BF),
            pltpu.VMEM(level, BF),
            pltpu.VMEM(level, BF),
            pltpu.VMEM((2, 2, ROWS, points), BF),
            pltpu.SemaphoreType.DMA((copies,)),
            pltpu.SemaphoreType.DMA((copies,)),
            pltpu.SemaphoreType.DMA((6,)),
        ]
        + [pltpu.VMEM(level[1:], BF)] * depth,
        compiler_params=pltpu.CompilerParams(
            collective_id=0, has_side_effects=True, vmem_limit_bytes=60 * 1024 * 1024
        ),
        name="operator",
    )(
        partner_perm.reshape(depth, boxes).T,
        coords.swapaxes(0, 1),
        *inputs,
    )
    return (out[0].reshape(fields.shape), out[1].reshape(fields.shape))


def solution(mesh):
    split = ("hi", "lo")
    in_specs = (
        P(split, None, None, None),
        P(split, None, None, None),
        P(split, None),
        P(split, None, None),
        P(split, None),
        P(None, split, None),
        P(split, None, None),
        P(split, None, None),
        P(None, split, None, None, None),
    )
    out_specs = (P(split, None, None, None), P(split, None, None, None))
    return jax.shard_map(body, mesh=mesh, in_specs=in_specs, out_specs=out_specs, check_vma=False)
```

```python
import functools
import math

import jax
import jax.numpy as jnp
import numpy as np
from jax import lax
from jax.experimental import pallas as pl
from jax.experimental.pallas import tpu as pltpu
from jax.sharding import PartitionSpec as P

WAVENUMBER = 9.0
SOFTENING = 0.1
MESH = pl.DeviceIdType.MESH
ROWS = 144
MAGIC = 12582912.0
BF = jnp.bfloat16
F32 = jnp.float32
NT = (((1,), (1,)), ((), ()))
TN = (((0,), (0,)), ((), ()))


ORDER = (
    "SF", "SZ1", "SB", "F0", "SYo", "B0", "F1", "RYo", "SXo", "RD", "RU", "B1", "F2", "NAo1",
    "NAo0", "B2", "Z", "SYm", "SZ2", "NAo2", "F3", "NAo3", "RYm", "SXm", "RZ2", "RXo", "SYt", "F4",
    "B3", "NAm0", "NAm1", "B4", "NEo", "F5", "NEm", "RYt", "NEt", "ES", "B5", "NAt2", "NAm2", "RXm",
    "F6", "NAt1", "B6", "SXt", "NAt3", "NAt0", "NAm3", "NCo", "NCm", "F7", "RXt", "NCt", "B7", "ER",
)


def fit(function, degree):
    nodes = 0.125 * (1.0 - np.cos(np.pi * (np.arange(400) + 0.5) / 400))
    poly = np.polynomial.chebyshev.Chebyshev.fit(nodes, function(nodes), degree, domain=[0, 0.25])
    return [float(c) for c in poly.convert(kind=np.polynomial.Polynomial).coef]


CYCLES = WAVENUMBER / (2 * math.pi)
COS_POLY = fit(lambda s: np.cos(2 * np.pi * np.sqrt(s)), 4)
SIN_POLY = fit(lambda s: np.sin(2 * np.pi * np.sqrt(s)) / np.sqrt(s), 3)


def horner(coefs, s):
    value = coefs[-1] * s + coefs[-2]
    for c in coefs[-3::-1]:
        value = value * s + c
    return value


def oscillation(squared, scale):
    w = squared * (CYCLES * CYCLES / 64.0) + CYCLES * CYCLES * SOFTENING * SOFTENING
    r = lax.rsqrt(w)
    y = w * r
    f = y - ((y + MAGIC) - MAGIC)
    s = f * f
    amp = scale * CYCLES
    real = horner([amp * c for c in COS_POLY], s) * r
    imag = horner([amp * c for c in SIN_POLY], s) * (f * r)
    return real.astype(BF), imag.astype(BF)


def spread(value, bits):
    total = 0
    for place, bit in enumerate(bits):
        total = total + (value // (1 << place)) % 2 * (1 << bit)
    return total


def dot(a, b, dims=None):
    if dims is None:
        return jnp.dot(a, b, preferred_element_type=F32)
    return lax.dot_general(a, b, dims, preferred_element_type=F32)


def kernel(
    n_hi, n_lo, scale,
    perm_ref, coords_ref, *refs,
):
    operands, refs = refs[:6], refs[6:]
    out_ref, adj_out_ref, *refs = refs
    (fields_ref, adj_ref, contrast_ref, lin_ref, lout_ref, mix_ref), refs = refs[:6], refs[6:]
    (
        grid, tgt, acc, ll_in, ll_out, blocks, fsend, bsend, brecv, carry, relays, res, exsend, exrecv,
        send_sem, recv_sem, load_sem, *frecv,
    ) = refs
    loads = [
        pltpu.make_async_copy(src, dst, load_sem.at[i])
        for i, (src, dst) in enumerate(
            zip(operands, (fields_ref, adj_ref, contrast_ref, lin_ref, lout_ref, mix_ref))
        )
    ]
    for load in loads:
        load.start()
    e = lax.axis_index("hi") * n_lo + lax.axis_index("lo")
    bits = (n_hi * n_lo).bit_length() - 1
    lo_bits = n_lo.bit_length() - 1
    levels = [b for b in range(bits) if b != lo_bits - 1]
    depth = len(levels)
    boxes = 4

    def where_is(device):
        return (device // n_lo, device % n_lo)

    def flip(bit):
        return e + (1 - 2 * ((e // (1 << bit)) % 2)) * (1 << bit)

    dims = []
    for d in range(3):
        own_bits = [t - 2 for t in range(2, bits + 2) if t % 3 == d]
        coord = 0
        for place, bit in enumerate(own_bits):
            coord = coord + (e // (1 << bit)) % 2 * (1 << place)
        rest = e - spread(coord, own_bits)
        dims.append((own_bits, coord, rest, 1 << len(own_bits)))

    def at(d, coordinate):
        own_bits, _, rest, _ = dims[d]
        return rest + spread(coordinate, own_bits)

    (_, xc, _, nx), (_, yc, _, ny), (_, zc, _, nz) = dims
    par = zc % 2
    mate = 2 - 2 * par
    third = 2 * par
    z_to = zc + 2 - 4 * par
    z_from = zc - 2 + 4 * par
    z_sends = jnp.logical_and(z_to >= 0, z_to < nz)
    z_receives = jnp.logical_and(z_from >= 0, z_from < nz)

    mirror = e // n_lo % 2
    xm = xc + mirror * (nx - 1 - 2 * xc)
    x_from, x_to = xc + 1 - 2 * mirror, xc - 1 + 2 * mirror
    imports, exports = xm < nx - 1, xm > 0
    far_edge, near_edge = (xm + 1) // nx, 1 - (xm + nx - 1) // nx

    def column(v):
        return v + mirror * (3 - 2 * v)

    ring_bits = list(range(lo_bits + 1, bits)) + [0]
    ring = 1 << len(ring_bits)
    zpos = 0
    for place, bit in enumerate(ring_bits):
        zpos = zpos + (e // (1 << bit)) % 2 * (1 << place)

    def on_ring(shift):
        return e - spread(zpos, ring_bits) + spread((zpos + ring + shift) % ring, ring_bits)

    def side(shift):
        return (zpos + ring + shift) % ring // (ring // 2)

    far_hop = ring // 2 - 1

    barrier = pltpu.get_barrier_semaphore()

    def greet(device):
        pl.semaphore_signal(barrier, inc=1, device_id=where_is(device), device_id_type=MESH)

    for bit in levels:
        greet(flip(bit))
    for shift in (far_hop, -far_hop, 1, -1):
        greet(on_ring(shift))
    others = []
    for d, n, c in ((0, nx, xc), (1, ny, yc)):
        others.append((c > 0, at(d, (c + n - 1) % n)))
        others.append((c < n - 1, at(d, (c + 1) % n)))
    others.append((z_sends, at(2, (z_to + nz) % nz)))
    others.append((z_receives, at(2, (z_from + nz) % nz)))
    for there, device in others:
        @pl.when(there)
        def _(device=device):
            greet(device)

    rank = lin_ref.shape[1]
    c = coords_ref[...].astype(F32)
    cells = jnp.floor(c)
    odd = cells - 2.0 * jnp.floor(0.5 * cells)
    raster = odd[0] + 2.0 * odd[1]
    c = c * 8.0
    norm = c[0] * c[0] + c[1] * c[1] + c[2] * c[2]
    high = jnp.floor(norm * (1.0 / 256.0)) * 256.0
    low = norm - high

    def holds(g, s):
        return raster[g : g + 1] == float(s)

    def pick(s, values):
        total = values[0]
        for g in range(1, boxes):
            total = jnp.where(holds(g, s), values[g], total)
        return total

    row = lax.broadcasted_iota(jnp.int32, (16, 128), 0)

    def stack(rows):
        value = jnp.zeros((16, 128), F32)
        for k, r in enumerate(rows):
            value = jnp.where(row == k, r, value)
        return value.astype(BF)

    one = jnp.ones((1, 128), F32)
    for s in range(boxes):
        x, y, z, h, w = (
            pick(s, [v[g : g + 1] for g in range(boxes)]) for v in (c[0], c[1], c[2], high, low)
        )
        grid[1, 1 + s // 2, 1 + s % 2, 128:144] = stack([x, y, z, h, w, one, one])
        tgt[s // 2 * 3 + column(1 + s % 2) - 1] = stack(
            [-2.0 * x, -2.0 * y, -2.0 * z, one, one, h, w]
        )

    for load in loads[:5]:
        load.wait()
    weighted = []
    for g in range(boxes):
        for ll, leaf in ((ll_in, lin_ref), (ll_out, lout_ref)):
            zero = jnp.zeros((rank, 128), BF)
            ll[g, 0:rank, 0:128] = leaf[g]
            ll[g, 0:rank, 128:256] = zero
            ll[g, rank : 2 * rank, 0:128] = zero
            ll[g, rank : 2 * rank, 128:256] = leaf[g]
        w = contrast_ref[g : g + 1, :] * fields_ref[g].astype(F32)
        weighted.append(w)
        lhs = jnp.concatenate([w[0:32], w[32:64]], axis=1).astype(BF)
        fsend[0, g] = dot(lhs, ll_in[g], NT).astype(BF)
    for s in range(boxes):
        place = (1, 1 + s // 2, 1 + s % 2)
        grid[place + (slice(0, 64),)] = pick(s, weighted).astype(BF)
        grid[place + (slice(64, 128),)] = pick(
            s, [adj_ref[g].astype(F32) for g in range(boxes)]
        ).astype(BF)

    loads[5].wait()

    def build(i, _):
        l, g = i // boxes, i % boxes
        zero = jnp.zeros((rank, rank), BF)
        for part in range(2):
            m = mix_ref[l, g, part]
            base = part * 128
            blocks[l, g, 0:rank, base : base + 128] = jnp.concatenate([m, zero], axis=1)
            blocks[l, g, rank : 2 * rank, base : base + 128] = jnp.concatenate([zero, m], axis=1)
        return 0

    lax.fori_loop(0, depth * boxes, build, 0)

    def inverse(l, s):
        found = 0
        for j in range(1, boxes):
            found = found + jnp.where(perm_ref[j, l] == s, j, 0)
        return jnp.minimum(found, boxes - 1)

    def back_products(l, backs):
        own = []
        for g in range(boxes):
            both = dot(backs[g], blocks[l, g])
            own.append(both[:, 0:128])
            carry[l, g] = both[:, 128:256].astype(BF)
        for s in range(boxes):
            bsend[l, s] = carry[l, inverse(l, s)]
        return own

    backs = []
    for g in range(boxes):
        a = adj_ref[g]
        lhs = jnp.concatenate([a[0:32], a[32:64]], axis=1)
        backs.append(dot(lhs, ll_out[g], NT).astype(BF))
    own_terms = back_products(depth - 1, backs)
    acc[...] = jnp.zeros_like(acc)

    def remote(src, dst, sem, device):
        return pltpu.make_async_remote_copy(
            src_ref=src, dst_ref=dst, send_sem=send_sem.at[sem], recv_sem=recv_sem.at[sem],
            device_id=where_is(device), device_id_type=MESH,
        )

    def forward_copy(l):
        return remote(fsend.at[l], frecv[l], l, flip(levels[l]))

    def back_copy(l):
        return remote(bsend.at[l], brecv.at[l], depth + l, flip(levels[l]))

    first_sem = 2 * depth
    last_sem = first_sem + 14
    up_first = remote(
        grid.at[1, 1, pl.ds(1, 2)], relays.at[0], first_sem, on_ring(far_hop)
    )
    down_first = remote(
        grid.at[1, 2, pl.ds(1, 2)], relays.at[1], last_sem, on_ring(-far_hop)
    )
    up_last = remote(
        relays.at[0], grid.at[2 * side(-far_hop), 1, pl.ds(1, 2)], last_sem + 1, on_ring(1)
    )
    down_last = remote(
        relays.at[1], grid.at[2 * side(far_hop), 2, pl.ds(1, 2)], last_sem + 2, on_ring(-1)
    )
    z2 = remote(
        grid.at[mate, pl.ds(1, 2), pl.ds(1, 2)],
        grid.at[third, pl.ds(1, 2), pl.ds(1, 2)],
        first_sem + 1, at(2, (z_to + nz) % nz),
    )

    def y_copies(plane, kind):
        sem = first_sem + 2 + 4 * kind
        up = remote(
            grid.at[plane, 2, pl.ds(1, 2)], grid.at[plane, 0, pl.ds(1, 2)],
            sem, at(1, (yc + 1) % ny),
        )
        down = remote(
            grid.at[plane, 1, pl.ds(1, 2)], grid.at[plane, 3, pl.ds(1, 2)],
            sem + 1, at(1, (yc + ny - 1) % ny),
        )
        return ((up, yc < ny - 1, yc > 0), (down, yc > 0, yc < ny - 1))

    def x_copies(plane, kind):
        copy = remote(
            grid.at[plane, pl.ds(0, 4), 1 + mirror], grid.at[plane, pl.ds(0, 4), 3 - 3 * mirror],
            first_sem + 4 + 4 * kind, at(0, (x_to + nx) % nx),
        )
        return ((copy, exports, imports),)

    extra = remote(exsend, exrecv, first_sem + 5, at(0, (x_from + nx) % nx))
    extra_copies = ((extra, imports, exports),)

    def start(copies):
        for copy, sends, _ in copies:
            @pl.when(sends)
            def _(copy=copy):
                copy.start()

    def arrive(copies):
        for copy, _, receives in copies:
            @pl.when(receives)
            def _(copy=copy):
                copy.wait_recv()

    def sent(copies):
        for copy, sends, _ in copies:
            @pl.when(sends)
            def _(copy=copy):
                copy.wait_send()

    own_y, own_x = y_copies(1, 0), x_copies(1, 0)
    mate_y, mate_x = y_copies(mate, 1), x_copies(mate, 1)
    third_y, third_x = y_copies(third, 2), x_copies(third, 2)
    z2_copies = ((z2, z_sends, z_receives),)

    y_low, y_high = 1 - (yc + ny - 1) // ny, (yc + 1) // ny
    third_or_own = jnp.where(z_receives, third, 1)
    rows_of = [y_low, 1, 2, 3 - y_high]

    def near(first, stride, count):
        def step(i, _):
            j = first + stride * i
            k, c = j // 6, j % 6
            plane = 1 + k % 2 * (mate - 1) + k // 2 * (third_or_own - 1)
            goal = (c + 4) // 6 + c // 5
            source = 1 + c % 2 + 2 * (c // 4) - 2 * (c // 5)
            x = column(source - far_edge * (c // 4 - c // 5))
            weight = (1 + near_edge * (1 - (c + 4) // 5)).astype(F32)
            for ty in range(2):
                target = tgt[3 * ty + goal]
                values, reals, imags = [], [], []
                for dy in range(3):
                    y = rows_of[ty + dy]
                    values.append(grid[plane, y, x, 0:128])
                    squared = dot(grid[plane, y, x, 128:144], target, TN)
                    real, imag = oscillation(squared, scale)
                    reals.append(real)
                    imags.append(imag)
                rhs = jnp.concatenate(
                    [jnp.concatenate(reals, axis=0), jnp.concatenate(imags, axis=0)], axis=1
                )
                product = dot(jnp.concatenate(values, axis=1), rhs)
                acc[3 * ty + goal] = acc[3 * ty + goal] + weight * product
            return 0

        lax.fori_loop(0, count, step, 0)

    def combine(a):
        ar, ai = a[:, 0:128], a[:, 128:256]
        return jnp.concatenate(
            [
                ar[0:32] - ai[32:64], ai[0:32] + ar[32:64],
                ar[64:96] + ai[96:128], ar[96:128] - ai[64:96],
            ],
            axis=0,
        )

    def neighbour_targets():
        for ty in range(2):
            f = grid[1, 1 + ty, 3 - 3 * mirror, 128:144].astype(F32)
            tgt[3 * ty + 2] = stack(
                [-2.0 * f[0:1], -2.0 * f[1:2], -2.0 * f[2:3], one, one, f[3:4], f[4:5]]
            )

    def send_extra():
        for ty in range(2):
            exsend[ty] = combine(acc[3 * ty + 2]).astype(BF)
        start(extra_copies)

    def receive_extra():
        for ty in range(2):
            for x in range(2):
                res[2 * ty + x] = combine(acc[3 * ty + column(1 + x) - 1])

        @pl.when(exports)
        def _():
            extra.wait_recv()
            for ty in range(2):
                mine = 2 * ty + mirror
                res[mine] = res[mine] + exrecv[ty].astype(F32)

    peers = depth + 4
    for there, _ in others:
        peers = peers + there.astype(jnp.int32)
    pl.semaphore_wait(barrier, peers)

    coefs = [fsend[0, g] for g in range(boxes)]

    def forward_step(i, coefs):
        mine = [dot(coefs[g], blocks[i, g, :, 0:128], NT) for g in range(boxes)]
        forward_copy(i).wait_recv()
        new = []
        for g in range(boxes):
            arrived = frecv[i][perm_ref[g, i]]
            c = (mine[g] + dot(arrived, blocks[i, g, :, 128:256], NT)).astype(BF)
            new.append(c)
            if i + 1 < depth:
                fsend[i + 1, g] = c
        if i + 1 < depth:
            forward_copy(i + 1).start()
        return new

    def back_step(i, own_terms):
        l = depth - 1 - i
        back_copy(l).wait_recv()
        backs = [(own_terms[g] + brecv[l, g].astype(F32)).astype(BF) for g in range(boxes)]
        if l > 0:
            own_terms = back_products(l - 1, backs)
            back_copy(l - 1).start()
        return backs, own_terms

    def when_third(action, *copies):
        @pl.when(z_receives)
        def _():
            for c in copies:
                action(c)

    def z_last():
        up_last.wait_recv()
        down_last.wait_recv()

    def relay(first, last):
        first.wait_recv()
        last.start()

    def own_columns():
        arrive(own_x)
        neighbour_targets()

    actions = {
        "SF": lambda: forward_copy(0).start(),
        "SB": lambda: back_copy(depth - 1).start(),
        "SYo": lambda: start(own_y), "RYo": lambda: arrive(own_y),
        "SXo": lambda: start(own_x), "RXo": own_columns,
        "SZ1": lambda: (up_first.start(), down_first.start()),
        "RU": lambda: relay(up_first, up_last), "RD": lambda: relay(down_first, down_last),
        "Z": z_last,
        "SYm": lambda: start(mate_y), "RYm": lambda: arrive(mate_y),
        "SXm": lambda: start(mate_x), "RXm": lambda: arrive(mate_x),
        "SZ2": lambda: start(z2_copies), "RZ2": lambda: arrive(z2_copies),
        "SYt": lambda: when_third(start, third_y), "RYt": lambda: when_third(arrive, third_y),
        "SXt": lambda: when_third(start, third_x), "RXt": lambda: when_third(arrive, third_x),
        "ES": send_extra, "ER": receive_extra,
    }
    pending = []

    def run_near():
        while pending:
            stride = pending[1] - pending[0] if len(pending) > 1 else 1
            count = 1
            while count < len(pending) and pending[count] - pending[count - 1] == stride:
                count += 1
            near(pending[0], stride, count)
            del pending[:count]

    for word in ORDER:
        if word[0] == "N":
            c = {"A": int(word[-1]) if word[-1].isdigit() else 0, "C": 4, "E": 5}[word[1]]
            pending.append("omt".index(word[2]) * 6 + c)
            continue
        run_near()
        if word[0] == "F":
            if int(word[1]) < depth:
                coefs = forward_step(int(word[1]), coefs)
        elif word[0] == "B":
            if int(word[1]) < depth:
                backs, own_terms = back_step(int(word[1]), own_terms)
        else:
            actions[word]()
    run_near()

    def pick_raster(g):
        total = res[0]
        for s in range(1, boxes):
            total = jnp.where(holds(g, s), res[s], total)
        return total

    for g in range(boxes):
        sums = pick_raster(g)
        far = dot(coefs[g], ll_out[g])
        out_ref[g, 0:32] = (
            fields_ref[g, 0:32].astype(F32) - (sums[0:32] + far[:, 0:128])
        ).astype(BF)
        out_ref[g, 32:64] = (
            fields_ref[g, 32:64].astype(F32) - (sums[32:64] + far[:, 128:256])
        ).astype(BF)
        far = dot(backs[g], ll_in[g])
        contrast = contrast_ref[g : g + 1, :]
        adj_out_ref[g, 0:32] = (
            adj_ref[g, 0:32].astype(F32) - contrast * (sums[64:96] + far[:, 0:128])
        ).astype(BF)
        adj_out_ref[g, 32:64] = (
            adj_ref[g, 32:64].astype(F32) - contrast * (sums[96:128] + far[:, 128:256])
        ).astype(BF)

    for l in range(depth):
        forward_copy(l).wait_send()
        back_copy(l).wait_send()
    up_first.wait_send()
    down_first.wait_send()
    up_last.wait_send()
    down_last.wait_send()
    sent(z2_copies)
    sent(own_y)
    sent(own_x)
    sent(mate_y)
    sent(mate_x)
    sent(extra_copies)

    @pl.when(z_receives)
    def _():
        sent(third_y)
        sent(third_x)


def body(fields, adjoint_in, contrast, coords, neighbours, partner_perm, leaf_in, leaf_out, mixing):
    boxes, parts, sides, points = fields.shape
    depth = mixing.shape[0]
    rank = leaf_in.shape[1]
    n_hi, n_lo = lax.axis_size("hi"), lax.axis_size("lo")
    scale = 1.0 / math.sqrt(27 * points)
    vmem = pl.BlockSpec(memory_space=pltpu.VMEM)
    smem = pl.BlockSpec(memory_space=pltpu.SMEM)
    away = pl.BlockSpec(memory_space=pl.ANY)
    flat = (boxes, parts * sides, points)
    copies = 2 * depth + 17
    level = (depth, boxes, sides, 2 * rank)
    inputs = (
        fields.reshape(flat), adjoint_in.reshape(flat), contrast, leaf_in, leaf_out, mixing,
    )
    out = pl.pallas_call(
        functools.partial(kernel, n_hi, n_lo, scale),
        out_shape=[jax.ShapeDtypeStruct(flat, BF)] * 2,
        in_specs=[smem, vmem] + [away] * 6,
        out_specs=[vmem] * 2,
        scratch_shapes=[pltpu.VMEM(v.shape, v.dtype) for v in inputs]
        + [
            pltpu.VMEM((3, 4, 4, ROWS, points), BF),
            pltpu.VMEM((6, 16, points), BF),
            pltpu.VMEM((6, 4 * sides, 2 * points), F32),
            pltpu.VMEM((boxes, 2 * rank, 2 * points), BF),
            pltpu.VMEM((boxes, 2 * rank, 2 * points), BF),
            pltpu.VMEM((depth, boxes, 2 * rank, 4 * rank), BF),
            pltpu.VMEM(level, BF),
            pltpu.VMEM(level, BF),
            pltpu.VMEM(level, BF),
            pltpu.VMEM(level, BF),
            pltpu.VMEM((2, 2, ROWS, points), BF),
            pltpu.VMEM((boxes, 4 * sides, points), F32),
            pltpu.VMEM((2, 4 * sides, points), BF),
            pltpu.VMEM((2, 4 * sides, points), BF),
            pltpu.SemaphoreType.DMA((copies,)),
            pltpu.SemaphoreType.DMA((copies,)),
            pltpu.SemaphoreType.DMA((6,)),
        ]
        + [pltpu.VMEM(level[1:], BF)] * depth,
        compiler_params=pltpu.CompilerParams(
            collective_id=0, has_side_effects=True, vmem_limit_bytes=60 * 1024 * 1024
        ),
        name="operator",
    )(
        partner_perm.reshape(depth, boxes).T,
        coords.swapaxes(0, 1),
        *inputs,
    )
    return (out[0].reshape(fields.shape), out[1].reshape(fields.shape))


def solution(mesh):
    split = ("hi", "lo")
    in_specs = (
        P(split, None, None, None),
        P(split, None, None, None),
        P(split, None),
        P(split, None, None),
        P(split, None),
        P(None, split, None),
        P(split, None, None),
        P(split, None, None),
        P(None, split, None, None, None),
    )
    out_specs = (P(split, None, None, None), P(split, None, None, None))
    return jax.shard_map(body, mesh=mesh, in_specs=in_specs, out_specs=out_specs, check_vma=False)
```

```python
import functools
import math

import jax
import jax.numpy as jnp
import numpy as np
from jax import lax
from jax.experimental import pallas as pl
from jax.experimental.pallas import tpu as pltpu
from jax.sharding import PartitionSpec as P

WAVENUMBER = 9.0
SOFTENING = 0.1
MESH = pl.DeviceIdType.MESH
ROWS = 144
MAGIC = 12582912.0
BF = jnp.bfloat16
F32 = jnp.float32
NT = (((1,), (1,)), ((), ()))
TN = (((0,), (0,)), ((), ()))


ORDER = (
    "SF", "SZ1", "SB", "F0", "SYo", "B0", "F1", "RYo", "SXo", "RD", "RU", "B1", "F2", "NAo1",
    "NAo0", "B2", "Z", "SYm", "SZ2", "NAo2", "F3", "NAo3", "RYm", "SXm", "RZ2", "RXo", "SYt", "F4",
    "B3", "NAm0", "NAm1", "B4", "NEo", "F5", "NEm", "RYt", "NEt", "ES", "B5", "NAt2", "NAm2", "RXm",
    "F6", "NAt1", "B6", "SXt", "NAt3", "NAt0", "NAm3", "NCo", "NCm", "F7", "RXt", "NCt", "B7", "ER",
)


def fit(function, degree):
    nodes = 0.125 * (1.0 - np.cos(np.pi * (np.arange(400) + 0.5) / 400))
    poly = np.polynomial.chebyshev.Chebyshev.fit(nodes, function(nodes), degree, domain=[0, 0.25])
    return [float(c) for c in poly.convert(kind=np.polynomial.Polynomial).coef]


CYCLES = WAVENUMBER / (2 * math.pi)
COS_POLY = fit(lambda s: np.cos(2 * np.pi * np.sqrt(s)), 4)
SIN_POLY = fit(lambda s: np.sin(2 * np.pi * np.sqrt(s)) / np.sqrt(s), 3)


def horner(coefs, s):
    value = coefs[-1] * s + coefs[-2]
    for c in coefs[-3::-1]:
        value = value * s + c
    return value


def oscillation(squared, scale):
    w = squared * (CYCLES * CYCLES / 64.0) + CYCLES * CYCLES * SOFTENING * SOFTENING
    r = lax.rsqrt(w)
    y = w * r
    f = y - ((y + MAGIC) - MAGIC)
    s = f * f
    amp = scale * CYCLES
    real = horner([amp * c for c in COS_POLY], s) * r
    imag = horner([amp * c for c in SIN_POLY], s) * (f * r)
    return real.astype(BF), imag.astype(BF)


def spread(value, bits):
    total = 0
    for place, bit in enumerate(bits):
        total = total + (value // (1 << place)) % 2 * (1 << bit)
    return total


def dot(a, b, dims=None):
    if dims is None:
        return jnp.dot(a, b, preferred_element_type=F32)
    return lax.dot_general(a, b, dims, preferred_element_type=F32)


def kernel(
    n_hi, n_lo, scale,
    perm_ref, coords_ref, *refs,
):
    operands, refs = refs[:6], refs[6:]
    out_ref, adj_out_ref, *refs = refs
    (fields_ref, adj_ref, contrast_ref, lin_ref, lout_ref, mix_ref), refs = refs[:6], refs[6:]
    (
        grid, tgt, acc, ll_in, ll_out, blocks, fsend, bsend, brecv, carry, relays, res, exsend, exrecv,
        send_sem, recv_sem, load_sem, *frecv,
    ) = refs
    loads = [
        pltpu.make_async_copy(src, dst, load_sem.at[i])
        for i, (src, dst) in enumerate(
            zip(operands, (fields_ref, adj_ref, contrast_ref, lin_ref, lout_ref, mix_ref))
        )
    ]
    for load in loads:
        load.start()
    e = lax.axis_index("hi") * n_lo + lax.axis_index("lo")
    bits = (n_hi * n_lo).bit_length() - 1
    lo_bits = n_lo.bit_length() - 1
    levels = [b for b in range(bits) if b != lo_bits - 1]
    depth = len(levels)
    boxes = 4

    def where_is(device):
        return (device // n_lo, device % n_lo)

    def flip(bit):
        return e + (1 - 2 * ((e // (1 << bit)) % 2)) * (1 << bit)

    dims = []
    for d in range(3):
        own_bits = [t - 2 for t in range(2, bits + 2) if t % 3 == d]
        coord = 0
        for place, bit in enumerate(own_bits):
            coord = coord + (e // (1 << bit)) % 2 * (1 << place)
        rest = e - spread(coord, own_bits)
        dims.append((own_bits, coord, rest, 1 << len(own_bits)))

    def at(d, coordinate):
        own_bits, _, rest, _ = dims[d]
        return rest + spread(coordinate, own_bits)

    (_, xc, _, nx), (_, yc, _, ny), (_, zc, _, nz) = dims
    par = zc % 2
    mate = 2 - 2 * par
    third = 2 * par
    z_to = zc + 2 - 4 * par
    z_from = zc - 2 + 4 * par
    z_sends = jnp.logical_and(z_to >= 0, z_to < nz)
    z_receives = jnp.logical_and(z_from >= 0, z_from < nz)

    mirror = e // n_lo % 2
    xm = xc + mirror * (nx - 1 - 2 * xc)
    x_from, x_to = xc + 1 - 2 * mirror, xc - 1 + 2 * mirror
    imports, exports = xm < nx - 1, xm > 0
    far_edge, near_edge = (xm + 1) // nx, 1 - (xm + nx - 1) // nx

    def column(v):
        return v + mirror * (3 - 2 * v)

    ring_bits = list(range(lo_bits + 1, bits)) + [0]
    ring = 1 << len(ring_bits)
    zpos = 0
    for place, bit in enumerate(ring_bits):
        zpos = zpos + (e // (1 << bit)) % 2 * (1 << place)

    def on_ring(shift):
        return e - spread(zpos, ring_bits) + spread((zpos + ring + shift) % ring, ring_bits)

    def side(shift):
        return (zpos + ring + shift) % ring // (ring // 2)

    far_hop = ring // 2 - 1

    barrier = pltpu.get_barrier_semaphore()

    def greet(device):
        pl.semaphore_signal(barrier, inc=1, device_id=where_is(device), device_id_type=MESH)

    for bit in levels:
        greet(flip(bit))
    for shift in (far_hop, -far_hop, 1, -1):
        greet(on_ring(shift))
    others = []
    for d, n, c in ((0, nx, xc), (1, ny, yc)):
        others.append((c > 0, at(d, (c + n - 1) % n)))
        others.append((c < n - 1, at(d, (c + 1) % n)))
    others.append((z_sends, at(2, (z_to + nz) % nz)))
    others.append((z_receives, at(2, (z_from + nz) % nz)))
    for there, device in others:
        @pl.when(there)
        def _(device=device):
            greet(device)

    rank = lin_ref.shape[1]
    c = coords_ref[...].astype(F32)
    cells = jnp.floor(c)
    odd = cells - 2.0 * jnp.floor(0.5 * cells)
    raster = odd[0] + 2.0 * odd[1]
    c = c * 8.0
    norm = c[0] * c[0] + c[1] * c[1] + c[2] * c[2]
    high = jnp.floor(norm * (1.0 / 256.0)) * 256.0
    low = norm - high

    def holds(g, s):
        return raster[g : g + 1] == float(s)

    def pick(s, values):
        total = values[0]
        for g in range(1, boxes):
            total = jnp.where(holds(g, s), values[g], total)
        return total

    row = lax.broadcasted_iota(jnp.int32, (16, 128), 0)

    def stack(rows):
        value = jnp.zeros((16, 128), F32)
        for k, r in enumerate(rows):
            value = jnp.where(row == k, r, value)
        return value.astype(BF)

    one = jnp.ones((1, 128), F32)
    for s in range(boxes):
        x, y, z, h, w = (
            pick(s, [v[g : g + 1] for g in range(boxes)]) for v in (c[0], c[1], c[2], high, low)
        )
        grid[1, 1 + s // 2, 1 + s % 2, 128:144] = stack([x, y, z, h, w, one, one])
        tgt[column(1 + s % 2) - 1, :, 128 * (s // 2) : 128 * (s // 2) + 128] = stack(
            [-2.0 * x, -2.0 * y, -2.0 * z, one, one, h, w]
        )

    def double(ll, leaf, g):
        zero = jnp.zeros((rank, 128), BF)
        ll[g, 0:rank, 0:128] = leaf[g]
        ll[g, 0:rank, 128:256] = zero
        ll[g, rank : 2 * rank, 0:128] = zero
        ll[g, rank : 2 * rank, 128:256] = leaf[g]

    for load in loads[:4]:
        load.wait()
    weighted = []
    for g in range(boxes):
        double(ll_in, lin_ref, g)
        w = contrast_ref[g : g + 1, :] * fields_ref[g].astype(F32)
        weighted.append(w)
        lhs = jnp.concatenate([w[0:32], w[32:64]], axis=1).astype(BF)
        fsend[0, g] = dot(lhs, ll_in[g], NT).astype(BF)
    for s in range(boxes):
        place = (1, 1 + s // 2, 1 + s % 2)
        grid[place + (slice(0, 64),)] = pick(s, weighted).astype(BF)
        grid[place + (slice(64, 128),)] = pick(
            s, [adj_ref[g].astype(F32) for g in range(boxes)]
        ).astype(BF)

    def build(i, _):
        l, g = i // boxes, i % boxes
        zero = jnp.zeros((rank, rank), BF)
        for part in range(2):
            m = mix_ref[l, g, part]
            base = part * 128
            blocks[l, g, 0:rank, base : base + 128] = jnp.concatenate([m, zero], axis=1)
            blocks[l, g, rank : 2 * rank, base : base + 128] = jnp.concatenate([zero, m], axis=1)
        return 0

    def inverse(l, s):
        found = 0
        for j in range(1, boxes):
            found = found + jnp.where(perm_ref[j, l] == s, j, 0)
        return jnp.minimum(found, boxes - 1)

    def back_products(l, backs):
        own = []
        for g in range(boxes):
            both = dot(backs[g], blocks[l, g])
            own.append(both[:, 0:128])
            carry[l, g] = both[:, 128:256].astype(BF)
        for s in range(boxes):
            bsend[l, s] = carry[l, inverse(l, s)]
        return own

    def first_back():
        loads[4].wait()
        loads[5].wait()
        lax.fori_loop((depth - 1) * boxes, depth * boxes, build, 0)
        backs = []
        for g in range(boxes):
            double(ll_out, lout_ref, g)
            a = adj_ref[g]
            lhs = jnp.concatenate([a[0:32], a[32:64]], axis=1)
            backs.append(dot(lhs, ll_out[g], NT).astype(BF))
        own_terms = back_products(depth - 1, backs)
        back_copy(depth - 1).start()
        lax.fori_loop(0, (depth - 1) * boxes, build, 0)
        acc[...] = jnp.zeros_like(acc)
        return own_terms


    def remote(src, dst, sem, device):
        return pltpu.make_async_remote_copy(
            src_ref=src, dst_ref=dst, send_sem=send_sem.at[sem], recv_sem=recv_sem.at[sem],
            device_id=where_is(device), device_id_type=MESH,
        )

    def forward_copy(l):
        return remote(fsend.at[l], frecv[l], l, flip(levels[l]))

    def back_copy(l):
        return remote(bsend.at[l], brecv.at[l], depth + l, flip(levels[l]))

    first_sem = 2 * depth
    last_sem = first_sem + 14
    up_first = remote(
        grid.at[1, 1, pl.ds(1, 2)], relays.at[0], first_sem, on_ring(far_hop)
    )
    down_first = remote(
        grid.at[1, 2, pl.ds(1, 2)], relays.at[1], last_sem, on_ring(-far_hop)
    )
    up_last = remote(
        relays.at[0], grid.at[2 * side(-far_hop), 1, pl.ds(1, 2)], last_sem + 1, on_ring(1)
    )
    down_last = remote(
        relays.at[1], grid.at[2 * side(far_hop), 2, pl.ds(1, 2)], last_sem + 2, on_ring(-1)
    )
    z2 = remote(
        grid.at[mate, pl.ds(1, 2), pl.ds(1, 2)],
        grid.at[third, pl.ds(1, 2), pl.ds(1, 2)],
        first_sem + 1, at(2, (z_to + nz) % nz),
    )

    def y_copies(plane, kind):
        sem = first_sem + 2 + 4 * kind
        up = remote(
            grid.at[plane, 2, pl.ds(1, 2)], grid.at[plane, 0, pl.ds(1, 2)],
            sem, at(1, (yc + 1) % ny),
        )
        down = remote(
            grid.at[plane, 1, pl.ds(1, 2)], grid.at[plane, 3, pl.ds(1, 2)],
            sem + 1, at(1, (yc + ny - 1) % ny),
        )
        return ((up, yc < ny - 1, yc > 0), (down, yc > 0, yc < ny - 1))

    def x_copies(plane, kind):
        copy = remote(
            grid.at[plane, pl.ds(0, 4), 1 + mirror], grid.at[plane, pl.ds(0, 4), 3 - 3 * mirror],
            first_sem + 4 + 4 * kind, at(0, (x_to + nx) % nx),
        )
        return ((copy, exports, imports),)

    extra = remote(exsend, exrecv, first_sem + 5, at(0, (x_from + nx) % nx))
    extra_copies = ((extra, imports, exports),)

    def start(copies):
        for copy, sends, _ in copies:
            @pl.when(sends)
            def _(copy=copy):
                copy.start()

    def arrive(copies):
        for copy, _, receives in copies:
            @pl.when(receives)
            def _(copy=copy):
                copy.wait_recv()

    def sent(copies):
        for copy, sends, _ in copies:
            @pl.when(sends)
            def _(copy=copy):
                copy.wait_send()

    own_y, own_x = y_copies(1, 0), x_copies(1, 0)
    mate_y, mate_x = y_copies(mate, 1), x_copies(mate, 1)
    third_y, third_x = y_copies(third, 2), x_copies(third, 2)
    z2_copies = ((z2, z_sends, z_receives),)

    y_low, y_high = 1 - (yc + ny - 1) // ny, (yc + 1) // ny
    third_or_own = jnp.where(z_receives, third, 1)
    rows_of = [y_low, 1, 2, 3 - y_high]

    def near(first, stride, count):
        def step(i, _):
            j = first + stride * i
            k, c = j // 6, j % 6
            plane = 1 + k % 2 * (mate - 1) + k // 2 * (third_or_own - 1)
            goal = (c + 4) // 6 + c // 5
            source = 1 + c % 2 + 2 * (c // 4) - 2 * (c // 5)
            x = column(source - far_edge * (c // 4 - c // 5))
            weight = (1 + near_edge * (1 - (c + 4) // 5)).astype(F32)
            features = [grid[plane, y, x, 128:144] for y in rows_of]
            squared = dot(jnp.concatenate(features, axis=1), tgt[goal], TN)
            values = [grid[plane, y, x, 0:128] for y in rows_of]
            for ty in range(2):
                real, imag = oscillation(
                    squared[128 * ty : 128 * ty + 384, 128 * ty : 128 * ty + 128], scale
                )
                product = dot(
                    jnp.concatenate(values[ty : ty + 3], axis=1),
                    jnp.concatenate([real, imag], axis=1),
                )
                acc[3 * ty + goal] = acc[3 * ty + goal] + weight * product
            return 0

        lax.fori_loop(0, count, step, 0)

    def combine(a):
        ar, ai = a[:, 0:128], a[:, 128:256]
        return jnp.concatenate(
            [
                ar[0:32] - ai[32:64], ai[0:32] + ar[32:64],
                ar[64:96] + ai[96:128], ar[96:128] - ai[64:96],
            ],
            axis=0,
        )

    def neighbour_targets():
        for ty in range(2):
            f = grid[1, 1 + ty, 3 - 3 * mirror, 128:144].astype(F32)
            tgt[2, :, 128 * ty : 128 * ty + 128] = stack(
                [-2.0 * f[0:1], -2.0 * f[1:2], -2.0 * f[2:3], one, one, f[3:4], f[4:5]]
            )

    def send_extra():
        for ty in range(2):
            exsend[ty] = combine(acc[3 * ty + 2]).astype(BF)
        start(extra_copies)

    def receive_extra():
        for ty in range(2):
            for x in range(2):
                res[2 * ty + x] = combine(acc[3 * ty + column(1 + x) - 1])

        @pl.when(exports)
        def _():
            extra.wait_recv()
            for ty in range(2):
                mine = 2 * ty + mirror
                res[mine] = res[mine] + exrecv[ty].astype(F32)

    peers = depth + 4
    for there, _ in others:
        peers = peers + there.astype(jnp.int32)
    pl.semaphore_wait(barrier, peers)

    coefs = [fsend[0, g] for g in range(boxes)]

    def forward_step(i, coefs):
        mine = [dot(coefs[g], blocks[i, g, :, 0:128], NT) for g in range(boxes)]
        forward_copy(i).wait_recv()
        new = []
        for g in range(boxes):
            arrived = frecv[i][perm_ref[g, i]]
            c = (mine[g] + dot(arrived, blocks[i, g, :, 128:256], NT)).astype(BF)
            new.append(c)
            if i + 1 < depth:
                fsend[i + 1, g] = c
        if i + 1 < depth:
            forward_copy(i + 1).start()
        return new

    def back_step(i, own_terms):
        l = depth - 1 - i
        back_copy(l).wait_recv()
        backs = [(own_terms[g] + brecv[l, g].astype(F32)).astype(BF) for g in range(boxes)]
        if l > 0:
            own_terms = back_products(l - 1, backs)
            back_copy(l - 1).start()
        return backs, own_terms

    def when_third(action, *copies):
        @pl.when(z_receives)
        def _():
            for c in copies:
                action(c)

    def z_last():
        up_last.wait_recv()
        down_last.wait_recv()

    def relay(first, last):
        first.wait_recv()
        last.start()

    def own_columns():
        arrive(own_x)
        neighbour_targets()

    actions = {
        "SF": lambda: forward_copy(0).start(),
        "SYo": lambda: start(own_y), "RYo": lambda: arrive(own_y),
        "SXo": lambda: start(own_x), "RXo": own_columns,
        "SZ1": lambda: (up_first.start(), down_first.start()),
        "RU": lambda: relay(up_first, up_last), "RD": lambda: relay(down_first, down_last),
        "Z": z_last,
        "SYm": lambda: start(mate_y), "RYm": lambda: arrive(mate_y),
        "SXm": lambda: start(mate_x), "RXm": lambda: arrive(mate_x),
        "SZ2": lambda: start(z2_copies), "RZ2": lambda: arrive(z2_copies),
        "SYt": lambda: when_third(start, third_y), "RYt": lambda: when_third(arrive, third_y),
        "SXt": lambda: when_third(start, third_x), "RXt": lambda: when_third(arrive, third_x),
        "ES": send_extra, "ER": receive_extra,
    }
    pending = []

    def run_near():
        while pending:
            stride = pending[1] - pending[0] if len(pending) > 1 else 1
            count = 1
            while count < len(pending) and pending[count] - pending[count - 1] == stride:
                count += 1
            near(pending[0], stride, count)
            del pending[:count]

    for word in ORDER:
        if word[0] == "N":
            c = {"A": int(word[-1]) if word[-1].isdigit() else 0, "C": 4, "E": 5}[word[1]]
            pending.append("omt".index(word[2]) * 6 + c)
            continue
        run_near()
        if word == "SB":
            own_terms = first_back()
        elif word[0] == "F":
            if int(word[1]) < depth:
                coefs = forward_step(int(word[1]), coefs)
        elif word[0] == "B":
            if int(word[1]) < depth:
                backs, own_terms = back_step(int(word[1]), own_terms)
        else:
            actions[word]()
    run_near()

    def pick_raster(g):
        total = res[0]
        for s in range(1, boxes):
            total = jnp.where(holds(g, s), res[s], total)
        return total

    for g in range(boxes):
        sums = pick_raster(g)
        far = dot(coefs[g], ll_out[g])
        out_ref[g, 0:32] = (
            fields_ref[g, 0:32].astype(F32) - (sums[0:32] + far[:, 0:128])
        ).astype(BF)
        out_ref[g, 32:64] = (
            fields_ref[g, 32:64].astype(F32) - (sums[32:64] + far[:, 128:256])
        ).astype(BF)
        far = dot(backs[g], ll_in[g])
        contrast = contrast_ref[g : g + 1, :]
        adj_out_ref[g, 0:32] = (
            adj_ref[g, 0:32].astype(F32) - contrast * (sums[64:96] + far[:, 0:128])
        ).astype(BF)
        adj_out_ref[g, 32:64] = (
            adj_ref[g, 32:64].astype(F32) - contrast * (sums[96:128] + far[:, 128:256])
        ).astype(BF)

    for l in range(depth):
        forward_copy(l).wait_send()
        back_copy(l).wait_send()
    up_first.wait_send()
    down_first.wait_send()
    up_last.wait_send()
    down_last.wait_send()
    sent(z2_copies)
    sent(own_y)
    sent(own_x)
    sent(mate_y)
    sent(mate_x)
    sent(extra_copies)

    @pl.when(z_receives)
    def _():
        sent(third_y)
        sent(third_x)


def body(fields, adjoint_in, contrast, coords, neighbours, partner_perm, leaf_in, leaf_out, mixing):
    boxes, parts, sides, points = fields.shape
    depth = mixing.shape[0]
    rank = leaf_in.shape[1]
    n_hi, n_lo = lax.axis_size("hi"), lax.axis_size("lo")
    scale = 1.0 / math.sqrt(27 * points)
    vmem = pl.BlockSpec(memory_space=pltpu.VMEM)
    smem = pl.BlockSpec(memory_space=pltpu.SMEM)
    away = pl.BlockSpec(memory_space=pl.ANY)
    flat = (boxes, parts * sides, points)
    copies = 2 * depth + 17
    level = (depth, boxes, sides, 2 * rank)
    inputs = (
        fields.reshape(flat), adjoint_in.reshape(flat), contrast, leaf_in, leaf_out, mixing,
    )
    out = pl.pallas_call(
        functools.partial(kernel, n_hi, n_lo, scale),
        out_shape=[jax.ShapeDtypeStruct(flat, BF)] * 2,
        in_specs=[smem, vmem] + [away] * 6,
        out_specs=[vmem] * 2,
        scratch_shapes=[pltpu.VMEM(v.shape, v.dtype) for v in inputs]
        + [
            pltpu.VMEM((3, 4, 4, ROWS, points), BF),
            pltpu.VMEM((3, 16, 2 * points), BF),
            pltpu.VMEM((6, 4 * sides, 2 * points), F32),
            pltpu.VMEM((boxes, 2 * rank, 2 * points), BF),
            pltpu.VMEM((boxes, 2 * rank, 2 * points), BF),
            pltpu.VMEM((depth, boxes, 2 * rank, 4 * rank), BF),
            pltpu.VMEM(level, BF),
            pltpu.VMEM(level, BF),
            pltpu.VMEM(level, BF),
            pltpu.VMEM(level, BF),
            pltpu.VMEM((2, 2, ROWS, points), BF),
            pltpu.VMEM((boxes, 4 * sides, points), F32),
            pltpu.VMEM((2, 4 * sides, points), BF),
            pltpu.VMEM((2, 4 * sides, points), BF),
            pltpu.SemaphoreType.DMA((copies,)),
            pltpu.SemaphoreType.DMA((copies,)),
            pltpu.SemaphoreType.DMA((6,)),
        ]
        + [pltpu.VMEM(level[1:], BF)] * depth,
        compiler_params=pltpu.CompilerParams(
            collective_id=0, has_side_effects=True, vmem_limit_bytes=60 * 1024 * 1024
        ),
        name="operator",
    )(
        partner_perm.reshape(depth, boxes).T,
        coords.swapaxes(0, 1),
        *inputs,
    )
    return (out[0].reshape(fields.shape), out[1].reshape(fields.shape))


def solution(mesh):
    split = ("hi", "lo")
    in_specs = (
        P(split, None, None, None),
        P(split, None, None, None),
        P(split, None),
        P(split, None, None),
        P(split, None),
        P(None, split, None),
        P(split, None, None),
        P(split, None, None),
        P(None, split, None, None, None),
    )
    out_specs = (P(split, None, None, None), P(split, None, None, None))
    return jax.shard_map(body, mesh=mesh, in_specs=in_specs, out_specs=out_specs, check_vma=False)
```

```python
import functools
import math

import jax
import jax.numpy as jnp
import numpy as np
from jax import lax
from jax.experimental import pallas as pl
from jax.experimental.pallas import tpu as pltpu
from jax.sharding import PartitionSpec as P

WAVENUMBER = 9.0
SOFTENING = 0.1
MESH = pl.DeviceIdType.MESH
ROWS = 144
MAGIC = 12582912.0
BF = jnp.bfloat16
F32 = jnp.float32
NT = (((1,), (1,)), ((), ()))
TN = (((0,), (0,)), ((), ()))


ORDER = (
    "SZ1", "SF", "SB", "F0", "SYo", "B0", "F1", "B1", "RYo", "SXo", "F2", "NAo1", "Z", "SZ2", "B2",
    "SYm", "NAo0", "NAo3", "NAo2", "F3", "B3", "RYm", "SXm", "RXo", "RZ2", "SYt", "F4", "NAm0",
    "NEm", "NAm1", "B4", "F5", "NEo", "RYt", "SXt", "NEt", "NAt1", "NAt2", "F6", "ES", "NCo", "B5",
    "NAm2", "NAm3", "NAt3", "RXm", "B6", "NAt0", "NCm", "F7", "RXt", "NCt", "B7", "ER",
)


def fit(function, degree):
    nodes = 0.125 * (1.0 - np.cos(np.pi * (np.arange(400) + 0.5) / 400))
    poly = np.polynomial.chebyshev.Chebyshev.fit(nodes, function(nodes), degree, domain=[0, 0.25])
    return [float(c) for c in poly.convert(kind=np.polynomial.Polynomial).coef]


CYCLES = WAVENUMBER / (2 * math.pi)
COS_POLY = fit(lambda s: np.cos(2 * np.pi * np.sqrt(s)), 4)
SIN_POLY = fit(lambda s: np.sin(2 * np.pi * np.sqrt(s)) / np.sqrt(s), 3)


def horner(coefs, s):
    value = coefs[-1] * s + coefs[-2]
    for c in coefs[-3::-1]:
        value = value * s + c
    return value


def oscillation(squared, scale):
    w = squared * (CYCLES * CYCLES / 64.0) + CYCLES * CYCLES * SOFTENING * SOFTENING
    r = lax.rsqrt(w)
    y = w * r
    f = y - ((y + MAGIC) - MAGIC)
    s = f * f
    amp = scale * CYCLES
    real = horner([amp * c for c in COS_POLY], s) * r
    imag = horner([amp * c for c in SIN_POLY], s) * (f * r)
    return real.astype(BF), imag.astype(BF)


def spread(value, bits):
    total = 0
    for place, bit in enumerate(bits):
        total = total + (value // (1 << place)) % 2 * (1 << bit)
    return total


def dot(a, b, dims=None):
    if dims is None:
        return jnp.dot(a, b, preferred_element_type=F32)
    return lax.dot_general(a, b, dims, preferred_element_type=F32)


def kernel(
    n_hi, n_lo, scale,
    perm_ref, coords_ref, *refs,
):
    operands, refs = refs[:6], refs[6:]
    out_ref, *refs = refs
    (fields_ref, adj_ref, contrast_ref, lin_ref, lout_ref, mix_ref), refs = refs[:6], refs[6:]
    (
        grid, tgt, acc, ll_in, ll_out, blocks, fsend, bsend, brecv, carry, res, exsend, exrecv,
        send_sem, recv_sem, load_sem, *frecv,
    ) = refs
    loads = [
        pltpu.make_async_copy(src, dst, load_sem.at[i])
        for i, (src, dst) in enumerate(
            zip(operands, (fields_ref, adj_ref, contrast_ref, lin_ref, lout_ref, mix_ref))
        )
    ]
    for load in loads:
        load.start()
    e = lax.axis_index("hi") * n_lo + lax.axis_index("lo")
    bits = (n_hi * n_lo).bit_length() - 1
    lo_bits = n_lo.bit_length() - 1
    levels = [b for b in range(bits) if b != lo_bits - 1]
    depth = len(levels)
    boxes = 4

    def where_is(device):
        return (device // n_lo, device % n_lo)

    def flip(bit):
        return e + (1 - 2 * ((e // (1 << bit)) % 2)) * (1 << bit)

    dims = []
    for d in range(3):
        own_bits = [t - 2 for t in range(2, bits + 2) if t % 3 == d]
        coord = 0
        for place, bit in enumerate(own_bits):
            coord = coord + (e // (1 << bit)) % 2 * (1 << place)
        rest = e - spread(coord, own_bits)
        dims.append((own_bits, coord, rest, 1 << len(own_bits)))

    def at(d, coordinate):
        own_bits, _, rest, _ = dims[d]
        return rest + spread(coordinate, own_bits)

    (_, xc, _, nx), (_, yc, _, ny), (_, zc, _, nz) = dims
    par = zc % 2
    mate = 2 - 2 * par
    third = 2 * par
    z_to = zc + 2 - 4 * par
    z_from = zc - 2 + 4 * par
    z_sends = jnp.logical_and(z_to >= 0, z_to < nz)
    z_receives = jnp.logical_and(z_from >= 0, z_from < nz)

    mirror = e // n_lo % 2
    xm = xc + mirror * (nx - 1 - 2 * xc)
    x_from, x_to = xc + 1 - 2 * mirror, xc - 1 + 2 * mirror
    imports, exports = xm < nx - 1, xm > 0
    far_edge, near_edge = (xm + 1) // nx, 1 - (xm + nx - 1) // nx

    def column(v):
        return v + mirror * (3 - 2 * v)

    barrier = pltpu.get_barrier_semaphore()

    def greet(device):
        pl.semaphore_signal(barrier, inc=1, device_id=where_is(device), device_id_type=MESH)

    for bit in levels:
        greet(flip(bit))
    others = []
    for d, n, c in ((0, nx, xc), (1, ny, yc)):
        others.append((c > 0, at(d, (c + n - 1) % n)))
        others.append((c < n - 1, at(d, (c + 1) % n)))
    others.append((z_sends, at(2, (z_to + nz) % nz)))
    others.append((z_receives, at(2, (z_from + nz) % nz)))
    for there, device in others:
        @pl.when(there)
        def _(device=device):
            greet(device)

    rank = lin_ref.shape[1]
    c = coords_ref[...].astype(F32)
    cells = jnp.floor(c)
    odd = cells - 2.0 * jnp.floor(0.5 * cells)
    raster = odd[0] + 2.0 * odd[1]
    c = c * 8.0
    norm = c[0] * c[0] + c[1] * c[1] + c[2] * c[2]
    high = jnp.floor(norm * (1.0 / 256.0)) * 256.0
    low = norm - high

    def holds(g, s):
        return raster[g : g + 1] == float(s)

    def pick(s, values):
        total = values[0]
        for g in range(1, boxes):
            total = jnp.where(holds(g, s), values[g], total)
        return total

    row = lax.broadcasted_iota(jnp.int32, (16, 128), 0)

    def stack(rows):
        value = jnp.zeros((16, 128), F32)
        for k, r in enumerate(rows):
            value = jnp.where(row == k, r, value)
        return value.astype(BF)

    one = jnp.ones((1, 128), F32)
    for s in range(boxes):
        x, y, z, h, w = (
            pick(s, [v[g : g + 1] for g in range(boxes)]) for v in (c[0], c[1], c[2], high, low)
        )
        grid[1, 1 + s // 2, 1 + s % 2, 128:144] = stack([x, y, z, h, w, one, one])
        tgt[column(1 + s % 2) - 1, :, 128 * (s // 2) : 128 * (s // 2) + 128] = stack(
            [-2.0 * x, -2.0 * y, -2.0 * z, one, one, h, w]
        )

    def double(ll, leaf, g):
        zero = jnp.zeros((rank, 128), BF)
        ll[g, 0:rank, 0:128] = leaf[g]
        ll[g, 0:rank, 128:256] = zero
        ll[g, rank : 2 * rank, 0:128] = zero
        ll[g, rank : 2 * rank, 128:256] = leaf[g]

    for load in loads[:4]:
        load.wait()
    weighted = []
    for g in range(boxes):
        double(ll_in, lin_ref, g)
        w = contrast_ref[g : g + 1, :] * fields_ref[g].astype(F32)
        weighted.append(w)
        lhs = jnp.concatenate([w[0:32], w[32:64]], axis=1).astype(BF)
        fsend[0, g] = dot(lhs, ll_in[g], NT).astype(BF)
    for s in range(boxes):
        place = (1, 1 + s // 2, 1 + s % 2)
        grid[place + (slice(0, 64),)] = pick(s, weighted).astype(BF)
        grid[place + (slice(64, 128),)] = pick(
            s, [adj_ref[g].astype(F32) for g in range(boxes)]
        ).astype(BF)

    def build(i, _):
        l, g = i // boxes, i % boxes
        zero = jnp.zeros((rank, rank), BF)
        for part in range(2):
            m = mix_ref[l, g, part]
            base = part * 128
            blocks[l, g, 0:rank, base : base + 128] = jnp.concatenate([m, zero], axis=1)
            blocks[l, g, rank : 2 * rank, base : base + 128] = jnp.concatenate([zero, m], axis=1)
        return 0

    def inverse(l, s):
        found = 0
        for j in range(1, boxes):
            found = found + jnp.where(perm_ref[j, l] == s, j, 0)
        return jnp.minimum(found, boxes - 1)

    def back_products(l, backs):
        own = []
        for g in range(boxes):
            both = dot(backs[g], blocks[l, g])
            own.append(both[:, 0:128])
            carry[l, g] = both[:, 128:256].astype(BF)
        for s in range(boxes):
            bsend[l, s] = carry[l, inverse(l, s)]
        return own

    def first_back():
        loads[4].wait()
        loads[5].wait()
        lax.fori_loop((depth - 1) * boxes, depth * boxes, build, 0)
        backs = []
        for g in range(boxes):
            double(ll_out, lout_ref, g)
            a = adj_ref[g]
            lhs = jnp.concatenate([a[0:32], a[32:64]], axis=1)
            backs.append(dot(lhs, ll_out[g], NT).astype(BF))
        own_terms = back_products(depth - 1, backs)
        back_copy(depth - 1).start()
        lax.fori_loop(0, (depth - 1) * boxes, build, 0)
        acc[...] = jnp.zeros_like(acc)
        return own_terms


    def remote(src, dst, sem, device):
        return pltpu.make_async_remote_copy(
            src_ref=src, dst_ref=dst, send_sem=send_sem.at[sem], recv_sem=recv_sem.at[sem],
            device_id=where_is(device), device_id_type=MESH,
        )

    def forward_copy(l):
        return remote(fsend.at[l], frecv[l], l, flip(levels[l]))

    def back_copy(l):
        return remote(bsend.at[l], brecv.at[l], depth + l, flip(levels[l]))

    first_sem = 2 * depth
    z1 = remote(
        grid.at[1, pl.ds(1, 2), pl.ds(1, 2)],
        grid.at[third, pl.ds(1, 2), pl.ds(1, 2)],
        first_sem, flip(0),
    )
    z2 = remote(
        grid.at[mate, pl.ds(1, 2), pl.ds(1, 2)],
        grid.at[third, pl.ds(1, 2), pl.ds(1, 2)],
        first_sem + 1, at(2, (z_to + nz) % nz),
    )

    def y_copies(plane, kind):
        sem = first_sem + 2 + 4 * kind
        up = remote(
            grid.at[plane, 2, pl.ds(1, 2)], grid.at[plane, 0, pl.ds(1, 2)],
            sem, at(1, (yc + 1) % ny),
        )
        down = remote(
            grid.at[plane, 1, pl.ds(1, 2)], grid.at[plane, 3, pl.ds(1, 2)],
            sem + 1, at(1, (yc + ny - 1) % ny),
        )
        return ((up, yc < ny - 1, yc > 0), (down, yc > 0, yc < ny - 1))

    def x_copies(plane, kind):
        copy = remote(
            grid.at[plane, pl.ds(0, 4), 1 + mirror], grid.at[plane, pl.ds(0, 4), 3 - 3 * mirror],
            first_sem + 4 + 4 * kind, at(0, (x_to + nx) % nx),
        )
        return ((copy, exports, imports),)

    extra = remote(exsend, exrecv, first_sem + 5, at(0, (x_from + nx) % nx))
    extra_copies = ((extra, imports, exports),)

    def start(copies):
        for copy, sends, _ in copies:
            @pl.when(sends)
            def _(copy=copy):
                copy.start()

    def arrive(copies):
        for copy, _, receives in copies:
            @pl.when(receives)
            def _(copy=copy):
                copy.wait_recv()

    def sent(copies):
        for copy, sends, _ in copies:
            @pl.when(sends)
            def _(copy=copy):
                copy.wait_send()

    own_y, own_x = y_copies(1, 0), x_copies(1, 0)
    mate_y, mate_x = y_copies(mate, 1), x_copies(mate, 1)
    third_y, third_x = y_copies(third, 2), x_copies(third, 2)
    z2_copies = ((z2, z_sends, z_receives),)

    y_low, y_high = 1 - (yc + ny - 1) // ny, (yc + 1) // ny
    third_or_own = jnp.where(z_receives, third, 1)
    rows_of = [y_low, 1, 2, 3 - y_high]

    def near(first, stride, count):
        def step(i, _):
            j = first + stride * i
            k, c = j // 6, j % 6
            plane = 1 + k % 2 * (mate - 1) + k // 2 * (third_or_own - 1)
            goal = (c + 4) // 6 + c // 5
            source = 1 + c % 2 + 2 * (c // 4) - 2 * (c // 5)
            x = column(source - far_edge * (c // 4 - c // 5))
            weight = (1 + near_edge * (1 - (c + 4) // 5)).astype(F32)
            features = [grid[plane, y, x, 128:144] for y in rows_of]
            squared = dot(jnp.concatenate(features, axis=1), tgt[goal], TN)
            values = [grid[plane, y, x, 0:128] for y in rows_of]
            for ty in range(2):
                real, imag = oscillation(
                    squared[128 * ty : 128 * ty + 384, 128 * ty : 128 * ty + 128], scale
                )
                product = dot(
                    jnp.concatenate(values[ty : ty + 3], axis=1),
                    jnp.concatenate([real, imag], axis=1),
                )
                acc[3 * ty + goal] = acc[3 * ty + goal] + weight * product
            return 0

        lax.fori_loop(0, count, step, 0)

    def combine(a):
        ar, ai = a[:, 0:128], a[:, 128:256]
        return jnp.concatenate(
            [
                ar[0:32] - ai[32:64], ai[0:32] + ar[32:64],
                ar[64:96] + ai[96:128], ar[96:128] - ai[64:96],
            ],
            axis=0,
        )

    def neighbour_targets():
        for ty in range(2):
            f = grid[1, 1 + ty, 3 - 3 * mirror, 128:144].astype(F32)
            tgt[2, :, 128 * ty : 128 * ty + 128] = stack(
                [-2.0 * f[0:1], -2.0 * f[1:2], -2.0 * f[2:3], one, one, f[3:4], f[4:5]]
            )

    def send_extra():
        for ty in range(2):
            exsend[ty] = combine(acc[3 * ty + 2]).astype(BF)
        start(extra_copies)

    def receive_extra():
        for ty in range(2):
            for x in range(2):
                res[2 * ty + x] = combine(acc[3 * ty + column(1 + x) - 1])

        @pl.when(exports)
        def _():
            extra.wait_recv()
            for ty in range(2):
                mine = 2 * ty + mirror
                res[mine] = res[mine] + exrecv[ty].astype(F32)

    peers = depth
    for there, _ in others:
        peers = peers + there.astype(jnp.int32)
    pl.semaphore_wait(barrier, peers)

    coefs = [fsend[0, g] for g in range(boxes)]

    def forward_step(i, coefs):
        mine = [dot(coefs[g], blocks[i, g, :, 0:128], NT) for g in range(boxes)]
        forward_copy(i).wait_recv()
        new = []
        for g in range(boxes):
            arrived = frecv[i][perm_ref[g, i]]
            c = (mine[g] + dot(arrived, blocks[i, g, :, 128:256], NT)).astype(BF)
            new.append(c)
            if i + 1 < depth:
                fsend[i + 1, g] = c
        if i + 1 < depth:
            forward_copy(i + 1).start()
        return new

    def back_step(i, own_terms):
        l = depth - 1 - i
        back_copy(l).wait_recv()
        backs = [(own_terms[g] + brecv[l, g].astype(F32)).astype(BF) for g in range(boxes)]
        if l > 0:
            own_terms = back_products(l - 1, backs)
            back_copy(l - 1).start()
        return backs, own_terms

    def when_third(action, *copies):
        @pl.when(z_receives)
        def _():
            for c in copies:
                action(c)

    def own_columns():
        arrive(own_x)
        neighbour_targets()

    actions = {
        "SF": lambda: forward_copy(0).start(),
        "SYo": lambda: start(own_y), "RYo": lambda: arrive(own_y),
        "SXo": lambda: start(own_x), "RXo": own_columns,
        "SZ1": lambda: z1.start(), "Z": lambda: z1.wait_recv(),
        "SYm": lambda: start(mate_y), "RYm": lambda: arrive(mate_y),
        "SXm": lambda: start(mate_x), "RXm": lambda: arrive(mate_x),
        "SZ2": lambda: start(z2_copies), "RZ2": lambda: arrive(z2_copies),
        "SYt": lambda: when_third(start, third_y), "RYt": lambda: when_third(arrive, third_y),
        "SXt": lambda: when_third(start, third_x), "RXt": lambda: when_third(arrive, third_x),
        "ES": send_extra, "ER": receive_extra,
    }
    pending = []

    def run_near():
        while pending:
            stride = pending[1] - pending[0] if len(pending) > 1 else 1
            count = 1
            while count < len(pending) and pending[count] - pending[count - 1] == stride:
                count += 1
            near(pending[0], stride, count)
            del pending[:count]

    for word in ORDER:
        if word[0] == "N":
            c = {"A": int(word[-1]) if word[-1].isdigit() else 0, "C": 4, "E": 5}[word[1]]
            pending.append("omt".index(word[2]) * 6 + c)
            continue
        run_near()
        if word == "SB":
            own_terms = first_back()
        elif word[0] == "F":
            if int(word[1]) < depth:
                coefs = forward_step(int(word[1]), coefs)
        elif word[0] == "B":
            if int(word[1]) < depth:
                backs, own_terms = back_step(int(word[1]), own_terms)
        else:
            actions[word]()
    run_near()

    def pick_raster(g):
        total = res[0]
        for s in range(1, boxes):
            total = jnp.where(holds(g, s), res[s], total)
        return total

    for g in range(boxes):
        sums = pick_raster(g)
        far = dot(coefs[g], ll_out[g])
        out_ref[g, 0:32] = (
            fields_ref[g, 0:32].astype(F32) - (sums[0:32] + far[:, 0:128])
        ).astype(BF)
        out_ref[g, 32:64] = (
            fields_ref[g, 32:64].astype(F32) - (sums[32:64] + far[:, 128:256])
        ).astype(BF)
        far = dot(backs[g], ll_in[g])
        contrast = contrast_ref[g : g + 1, :]
        out_ref[boxes + g, 0:32] = (
            adj_ref[g, 0:32].astype(F32) - contrast * (sums[64:96] + far[:, 0:128])
        ).astype(BF)
        out_ref[boxes + g, 32:64] = (
            adj_ref[g, 32:64].astype(F32) - contrast * (sums[96:128] + far[:, 128:256])
        ).astype(BF)

    for l in range(depth):
        forward_copy(l).wait_send()
        back_copy(l).wait_send()
    z1.wait_send()
    sent(z2_copies)
    sent(own_y)
    sent(own_x)
    sent(mate_y)
    sent(mate_x)
    sent(extra_copies)

    @pl.when(z_receives)
    def _():
        sent(third_y)
        sent(third_x)


def body(fields, adjoint_in, contrast, coords, neighbours, partner_perm, leaf_in, leaf_out, mixing):
    boxes, parts, sides, points = fields.shape
    depth = mixing.shape[0]
    rank = leaf_in.shape[1]
    n_hi, n_lo = lax.axis_size("hi"), lax.axis_size("lo")
    scale = 1.0 / math.sqrt(27 * points)
    vmem = pl.BlockSpec(memory_space=pltpu.VMEM)
    smem = pl.BlockSpec(memory_space=pltpu.SMEM)
    away = pl.BlockSpec(memory_space=pl.ANY)
    flat = (boxes, parts * sides, points)
    copies = 2 * depth + 14
    level = (depth, boxes, sides, 2 * rank)
    inputs = (
        fields.reshape(flat), adjoint_in.reshape(flat), contrast, leaf_in, leaf_out, mixing,
    )
    out = pl.pallas_call(
        functools.partial(kernel, n_hi, n_lo, scale),
        out_shape=jax.ShapeDtypeStruct((2 * boxes,) + flat[1:], BF),
        in_specs=[smem, vmem] + [away] * 6,
        out_specs=vmem,
        scratch_shapes=[pltpu.VMEM(v.shape, v.dtype) for v in inputs]
        + [
            pltpu.VMEM((3, 4, 4, ROWS, points), BF),
            pltpu.VMEM((3, 16, 2 * points), BF),
            pltpu.VMEM((6, 4 * sides, 2 * points), F32),
            pltpu.VMEM((boxes, 2 * rank, 2 * points), BF),
            pltpu.VMEM((boxes, 2 * rank, 2 * points), BF),
            pltpu.VMEM((depth, boxes, 2 * rank, 4 * rank), BF),
            pltpu.VMEM(level, BF),
            pltpu.VMEM(level, BF),
            pltpu.VMEM(level, BF),
            pltpu.VMEM(level, BF),
            pltpu.VMEM((boxes, 4 * sides, points), F32),
            pltpu.VMEM((2, 4 * sides, points), BF),
            pltpu.VMEM((2, 4 * sides, points), BF),
            pltpu.SemaphoreType.DMA((copies,)),
            pltpu.SemaphoreType.DMA((copies,)),
            pltpu.SemaphoreType.DMA((6,)),
        ]
        + [pltpu.VMEM(level[1:], BF)] * depth,
        compiler_params=pltpu.CompilerParams(
            collective_id=0, has_side_effects=True, vmem_limit_bytes=60 * 1024 * 1024
        ),
        name="operator",
    )(
        partner_perm.reshape(depth, boxes).T,
        coords.swapaxes(0, 1),
        *inputs,
    )
    return (out[:boxes].reshape(fields.shape), out[boxes:].reshape(fields.shape))


def solution(mesh):
    split = ("hi", "lo")
    in_specs = (
        P(split, None, None, None),
        P(split, None, None, None),
        P(split, None),
        P(split, None, None),
        P(split, None),
        P(None, split, None),
        P(split, None, None),
        P(split, None, None),
        P(None, split, None, None, None),
    )
    out_specs = (P(split, None, None, None), P(split, None, None, None))
    return jax.shard_map(body, mesh=mesh, in_specs=in_specs, out_specs=out_specs, check_vma=False)
```

```python
import functools
import math

import jax
import jax.numpy as jnp
import numpy as np
from jax import lax
from jax.experimental import pallas as pl
from jax.experimental.pallas import tpu as pltpu
from jax.sharding import PartitionSpec as P

WAVENUMBER = 9.0
SOFTENING = 0.1
MESH = pl.DeviceIdType.MESH
ROWS = 144
MAGIC = 12582912.0
BF = jnp.bfloat16
F32 = jnp.float32
NT = (((1,), (1,)), ((), ()))
TN = (((0,), (0,)), ((), ()))


ORDER = (
    "SZ1", "SF", "SB", "FR", "SYo", "B0", "F0", "F1", "RYo", "SXo", "RD", "RU", "B1", "F2", "NAo1",
    "B2", "Z", "SZ2", "SYm", "NAo0", "B3", "NAo2", "F3", "NAo3", "RYm", "SXm", "RZ2", "SYt", "F4",
    "NAm2", "RXo", "NAm0", "NAm3", "NAm1", "B4", "F5", "NEo", "RYt", "SXt", "NEt", "NEm", "B5",
    "F6", "NAt2", "NAt1", "B6", "NAt3", "RXm", "NAt0", "ES", "NCo", "NCm", "BR", "F7", "RXt", "NCt",
    "B7", "ER",
)


def fit(function, degree):
    nodes = 0.125 * (1.0 - np.cos(np.pi * (np.arange(400) + 0.5) / 400))
    poly = np.polynomial.chebyshev.Chebyshev.fit(nodes, function(nodes), degree, domain=[0, 0.25])
    return [float(c) for c in poly.convert(kind=np.polynomial.Polynomial).coef]


CYCLES = WAVENUMBER / (2 * math.pi)
COS_POLY = fit(lambda s: np.cos(2 * np.pi * np.sqrt(s)), 4)
SIN_POLY = fit(lambda s: np.sin(2 * np.pi * np.sqrt(s)) / np.sqrt(s), 3)


def horner(coefs, s):
    value = coefs[-1] * s + coefs[-2]
    for c in coefs[-3::-1]:
        value = value * s + c
    return value


def oscillation(squared, scale):
    w = squared * (CYCLES * CYCLES / 64.0) + CYCLES * CYCLES * SOFTENING * SOFTENING
    r = lax.rsqrt(w)
    y = w * r
    f = y - ((y + MAGIC) - MAGIC)
    s = f * f
    amp = scale * CYCLES
    real = horner([amp * c for c in COS_POLY], s) * r
    imag = horner([amp * c for c in SIN_POLY], s) * (f * r)
    return real.astype(BF), imag.astype(BF)


def spread(value, bits):
    total = 0
    for place, bit in enumerate(bits):
        total = total + (value // (1 << place)) % 2 * (1 << bit)
    return total


def dot(a, b, dims=None):
    if dims is None:
        return jnp.dot(a, b, preferred_element_type=F32)
    return lax.dot_general(a, b, dims, preferred_element_type=F32)


def kernel(
    n_hi, n_lo, scale,
    perm_ref, coords_ref, *refs,
):
    operands, refs = refs[:6], refs[6:]
    out_ref, *refs = refs
    (fields_ref, adj_ref, contrast_ref, lin_ref, lout_ref, mix_ref), refs = refs[:6], refs[6:]
    (
        grid, tgt, acc, ll_in, ll_out, blocks, fsend, bsend, brecv, carry, relays, f_stop, b_stop, res, exsend, exrecv,
        send_sem, recv_sem, load_sem, *frecv,
    ) = refs
    loads = [
        pltpu.make_async_copy(src, dst, load_sem.at[i])
        for i, (src, dst) in enumerate(
            zip(operands, (fields_ref, adj_ref, contrast_ref, lin_ref, lout_ref, mix_ref))
        )
    ]
    for load in loads:
        load.start()
    e = lax.axis_index("hi") * n_lo + lax.axis_index("lo")
    bits = (n_hi * n_lo).bit_length() - 1
    lo_bits = n_lo.bit_length() - 1
    levels = [b for b in range(bits) if b != lo_bits - 1]
    depth = len(levels)
    boxes = 4

    def where_is(device):
        return (device // n_lo, device % n_lo)

    def flip(bit):
        return e + (1 - 2 * ((e // (1 << bit)) % 2)) * (1 << bit)

    dims = []
    for d in range(3):
        own_bits = [t - 2 for t in range(2, bits + 2) if t % 3 == d]
        coord = 0
        for place, bit in enumerate(own_bits):
            coord = coord + (e // (1 << bit)) % 2 * (1 << place)
        rest = e - spread(coord, own_bits)
        dims.append((own_bits, coord, rest, 1 << len(own_bits)))

    def at(d, coordinate):
        own_bits, _, rest, _ = dims[d]
        return rest + spread(coordinate, own_bits)

    (_, xc, _, nx), (_, yc, _, ny), (_, zc, _, nz) = dims
    par = zc % 2
    mate = 2 - 2 * par
    third = 2 * par
    z_to = zc + 2 - 4 * par
    z_from = zc - 2 + 4 * par
    z_sends = jnp.logical_and(z_to >= 0, z_to < nz)
    z_receives = jnp.logical_and(z_from >= 0, z_from < nz)

    mirror = e // n_lo % 2
    xm = xc + mirror * (nx - 1 - 2 * xc)
    x_from, x_to = xc + 1 - 2 * mirror, xc - 1 + 2 * mirror
    imports, exports = xm < nx - 1, xm > 0
    far_edge, near_edge = (xm + 1) // nx, 1 - (xm + nx - 1) // nx

    def column(v):
        return v + mirror * (3 - 2 * v)

    ring_bits = list(range(lo_bits + 1, bits)) + [0]
    ring = 1 << len(ring_bits)
    zpos = 0
    for place, bit in enumerate(ring_bits):
        zpos = zpos + (e // (1 << bit)) % 2 * (1 << place)

    def on_ring(shift):
        return e - spread(zpos, ring_bits) + spread((zpos + ring + shift) % ring, ring_bits)

    def side(shift):
        return (zpos + ring + shift) % ring // (ring // 2)

    far_hop = ring // 2 - 1

    barrier = pltpu.get_barrier_semaphore()

    def greet(device):
        pl.semaphore_signal(barrier, inc=1, device_id=where_is(device), device_id_type=MESH)

    for bit in levels:
        greet(flip(bit))
    for shift in (far_hop, -far_hop, 1, -1):
        greet(on_ring(shift))
    others = []
    for d, n, c in ((0, nx, xc), (1, ny, yc)):
        others.append((c > 0, at(d, (c + n - 1) % n)))
        others.append((c < n - 1, at(d, (c + 1) % n)))
    others.append((z_sends, at(2, (z_to + nz) % nz)))
    others.append((z_receives, at(2, (z_from + nz) % nz)))
    for there, device in others:
        @pl.when(there)
        def _(device=device):
            greet(device)

    rank = lin_ref.shape[1]
    c = coords_ref[...].astype(F32)
    cells = jnp.floor(c)
    odd = cells - 2.0 * jnp.floor(0.5 * cells)
    raster = odd[0] + 2.0 * odd[1]
    c = c * 8.0
    norm = c[0] * c[0] + c[1] * c[1] + c[2] * c[2]
    high = jnp.floor(norm * (1.0 / 256.0)) * 256.0
    low = norm - high

    def holds(g, s):
        return raster[g : g + 1] == float(s)

    def pick(s, values):
        total = values[0]
        for g in range(1, boxes):
            total = jnp.where(holds(g, s), values[g], total)
        return total

    row = lax.broadcasted_iota(jnp.int32, (16, 128), 0)

    def stack(rows):
        value = jnp.zeros((16, 128), F32)
        for k, r in enumerate(rows):
            value = jnp.where(row == k, r, value)
        return value.astype(BF)

    one = jnp.ones((1, 128), F32)
    for s in range(boxes):
        x, y, z, h, w = (
            pick(s, [v[g : g + 1] for g in range(boxes)]) for v in (c[0], c[1], c[2], high, low)
        )
        grid[1, 1 + s // 2, 1 + s % 2, 128:144] = stack([x, y, z, h, w, one, one])
        tgt[column(1 + s % 2) - 1, :, 128 * (s // 2) : 128 * (s // 2) + 128] = stack(
            [-2.0 * x, -2.0 * y, -2.0 * z, one, one, h, w]
        )

    def double(ll, leaf, g):
        zero = jnp.zeros((rank, 128), BF)
        ll[g, 0:rank, 0:128] = leaf[g]
        ll[g, 0:rank, 128:256] = zero
        ll[g, rank : 2 * rank, 0:128] = zero
        ll[g, rank : 2 * rank, 128:256] = leaf[g]

    for load in loads[:4]:
        load.wait()
    weighted = []
    for g in range(boxes):
        double(ll_in, lin_ref, g)
        w = contrast_ref[g : g + 1, :] * fields_ref[g].astype(F32)
        weighted.append(w)
        lhs = jnp.concatenate([w[0:32], w[32:64]], axis=1).astype(BF)
        fsend[0, g] = dot(lhs, ll_in[g], NT).astype(BF)
    for s in range(boxes):
        place = (1, 1 + s // 2, 1 + s % 2)
        grid[place + (slice(0, 64),)] = pick(s, weighted).astype(BF)
        grid[place + (slice(64, 128),)] = pick(
            s, [adj_ref[g].astype(F32) for g in range(boxes)]
        ).astype(BF)

    def build(i, _):
        l, g = i // boxes, i % boxes
        zero = jnp.zeros((rank, rank), BF)
        for part in range(2):
            m = mix_ref[l, g, part]
            base = part * 128
            blocks[l, g, 0:rank, base : base + 128] = jnp.concatenate([m, zero], axis=1)
            blocks[l, g, rank : 2 * rank, base : base + 128] = jnp.concatenate([zero, m], axis=1)
        return 0

    def inverse(l, s):
        found = 0
        for j in range(1, boxes):
            found = found + jnp.where(perm_ref[j, l] == s, j, 0)
        return jnp.minimum(found, boxes - 1)

    def back_products(l, backs):
        own = []
        for g in range(boxes):
            both = dot(backs[g], blocks[l, g])
            own.append(both[:, 0:128])
            carry[l, g] = both[:, 128:256].astype(BF)
        for s in range(boxes):
            bsend[l, s] = carry[l, inverse(l, s)]
        return own

    def first_back():
        loads[4].wait()
        loads[5].wait()
        lax.fori_loop((depth - 1) * boxes, depth * boxes, build, 0)
        backs = []
        for g in range(boxes):
            double(ll_out, lout_ref, g)
            a = adj_ref[g]
            lhs = jnp.concatenate([a[0:32], a[32:64]], axis=1)
            backs.append(dot(lhs, ll_out[g], NT).astype(BF))
        own_terms = back_products(depth - 1, backs)
        back_copy(depth - 1).start()
        lax.fori_loop(0, (depth - 1) * boxes, build, 0)
        acc[...] = jnp.zeros_like(acc)
        return own_terms


    def remote(src, dst, sem, device):
        return pltpu.make_async_remote_copy(
            src_ref=src, dst_ref=dst, send_sem=send_sem.at[sem], recv_sem=recv_sem.at[sem],
            device_id=where_is(device), device_id_type=MESH,
        )

    def forward_copy(l):
        return remote(fsend.at[l], frecv[l], l, flip(levels[l]))

    def back_copy(l):
        return remote(bsend.at[l], brecv.at[l], depth + l, flip(levels[l]))

    first_sem = 2 * depth
    last_sem = first_sem + 14
    up_first = remote(
        grid.at[1, 1, pl.ds(1, 2)], relays.at[0], first_sem, on_ring(far_hop)
    )
    down_first = remote(
        grid.at[1, 2, pl.ds(1, 2)], relays.at[1], last_sem, on_ring(-far_hop)
    )
    up_last = remote(
        relays.at[0], grid.at[2 * side(-far_hop), 1, pl.ds(1, 2)], last_sem + 1, on_ring(1)
    )
    down_last = remote(
        relays.at[1], grid.at[2 * side(far_hop), 2, pl.ds(1, 2)], last_sem + 2, on_ring(-1)
    )
    half = boxes // 2

    def halves(src, stop, dst, sem):
        first = (
            remote(src.at[pl.ds(0, half)], stop.at[0], sem, on_ring(far_hop)),
            remote(src.at[pl.ds(half, half)], stop.at[1], sem + 1, on_ring(-far_hop)),
        )
        last = (
            remote(stop.at[0], dst.at[pl.ds(0, half)], sem + 2, on_ring(1)),
            remote(stop.at[1], dst.at[pl.ds(half, half)], sem + 3, on_ring(-1)),
        )
        return first, last

    f_first, f_last = halves(fsend.at[0], f_stop, frecv[0], last_sem + 3)
    b_first, b_last = halves(bsend.at[0], b_stop, brecv.at[0], last_sem + 7)

    def start_all(copies):
        for copy in copies:
            copy.start()

    def arrive_all(copies):
        for copy in copies:
            copy.wait_recv()

    def relay_all(first, last):
        for before, after in zip(first, last):
            before.wait_recv()
            after.start()

    z2 = remote(
        grid.at[mate, pl.ds(1, 2), pl.ds(1, 2)],
        grid.at[third, pl.ds(1, 2), pl.ds(1, 2)],
        first_sem + 1, at(2, (z_to + nz) % nz),
    )

    def y_copies(plane, kind):
        sem = first_sem + 2 + 4 * kind
        up = remote(
            grid.at[plane, 2, pl.ds(1, 2)], grid.at[plane, 0, pl.ds(1, 2)],
            sem, at(1, (yc + 1) % ny),
        )
        down = remote(
            grid.at[plane, 1, pl.ds(1, 2)], grid.at[plane, 3, pl.ds(1, 2)],
            sem + 1, at(1, (yc + ny - 1) % ny),
        )
        return ((up, yc < ny - 1, yc > 0), (down, yc > 0, yc < ny - 1))

    def x_copies(plane, kind):
        copy = remote(
            grid.at[plane, pl.ds(0, 4), 1 + mirror], grid.at[plane, pl.ds(0, 4), 3 - 3 * mirror],
            first_sem + 4 + 4 * kind, at(0, (x_to + nx) % nx),
        )
        return ((copy, exports, imports),)

    extra = remote(exsend, exrecv, first_sem + 5, at(0, (x_from + nx) % nx))
    extra_copies = ((extra, imports, exports),)

    def start(copies):
        for copy, sends, _ in copies:
            @pl.when(sends)
            def _(copy=copy):
                copy.start()

    def arrive(copies):
        for copy, _, receives in copies:
            @pl.when(receives)
            def _(copy=copy):
                copy.wait_recv()

    def sent(copies):
        for copy, sends, _ in copies:
            @pl.when(sends)
            def _(copy=copy):
                copy.wait_send()

    own_y, own_x = y_copies(1, 0), x_copies(1, 0)
    mate_y, mate_x = y_copies(mate, 1), x_copies(mate, 1)
    third_y, third_x = y_copies(third, 2), x_copies(third, 2)
    z2_copies = ((z2, z_sends, z_receives),)

    y_low, y_high = 1 - (yc + ny - 1) // ny, (yc + 1) // ny
    third_or_own = jnp.where(z_receives, third, 1)
    rows_of = [y_low, 1, 2, 3 - y_high]

    def near(first, stride, count):
        def step(i, _):
            j = first + stride * i
            k, c = j // 6, j % 6
            plane = 1 + k % 2 * (mate - 1) + k // 2 * (third_or_own - 1)
            goal = (c + 4) // 6 + c // 5
            source = 1 + c % 2 + 2 * (c // 4) - 2 * (c // 5)
            x = column(source - far_edge * (c // 4 - c // 5))
            weight = (1 + near_edge * (1 - (c + 4) // 5)).astype(F32)
            features = [grid[plane, y, x, 128:144] for y in rows_of]
            squared = dot(jnp.concatenate(features, axis=1), tgt[goal], TN)
            values = [grid[plane, y, x, 0:128] for y in rows_of]
            for ty in range(2):
                real, imag = oscillation(
                    squared[128 * ty : 128 * ty + 384, 128 * ty : 128 * ty + 128], scale
                )
                product = dot(
                    jnp.concatenate(values[ty : ty + 3], axis=1),
                    jnp.concatenate([real, imag], axis=1),
                )
                acc[3 * ty + goal] = acc[3 * ty + goal] + weight * product
            return 0

        lax.fori_loop(0, count, step, 0)

    def combine(a):
        ar, ai = a[:, 0:128], a[:, 128:256]
        return jnp.concatenate(
            [
                ar[0:32] - ai[32:64], ai[0:32] + ar[32:64],
                ar[64:96] + ai[96:128], ar[96:128] - ai[64:96],
            ],
            axis=0,
        )

    def neighbour_targets():
        for ty in range(2):
            f = grid[1, 1 + ty, 3 - 3 * mirror, 128:144].astype(F32)
            tgt[2, :, 128 * ty : 128 * ty + 128] = stack(
                [-2.0 * f[0:1], -2.0 * f[1:2], -2.0 * f[2:3], one, one, f[3:4], f[4:5]]
            )

    def send_extra():
        for ty in range(2):
            exsend[ty] = combine(acc[3 * ty + 2]).astype(BF)
        start(extra_copies)

    def receive_extra():
        for ty in range(2):
            for x in range(2):
                res[2 * ty + x] = combine(acc[3 * ty + column(1 + x) - 1])

        @pl.when(exports)
        def _():
            extra.wait_recv()
            for ty in range(2):
                mine = 2 * ty + mirror
                res[mine] = res[mine] + exrecv[ty].astype(F32)

    peers = depth + 4
    for there, _ in others:
        peers = peers + there.astype(jnp.int32)
    pl.semaphore_wait(barrier, peers)

    coefs = [fsend[0, g] for g in range(boxes)]

    def forward_step(i, coefs):
        mine = [dot(coefs[g], blocks[i, g, :, 0:128], NT) for g in range(boxes)]
        if i == 0:
            arrive_all(f_last)
        else:
            forward_copy(i).wait_recv()
        new = []
        for g in range(boxes):
            arrived = frecv[i][perm_ref[g, i]]
            c = (mine[g] + dot(arrived, blocks[i, g, :, 128:256], NT)).astype(BF)
            new.append(c)
            if i + 1 < depth:
                fsend[i + 1, g] = c
        if i + 1 < depth:
            forward_copy(i + 1).start()
        return new

    def back_step(i, own_terms):
        l = depth - 1 - i
        if l == 0:
            arrive_all(b_last)
        else:
            back_copy(l).wait_recv()
        backs = [(own_terms[g] + brecv[l, g].astype(F32)).astype(BF) for g in range(boxes)]
        if l > 0:
            own_terms = back_products(l - 1, backs)
            if l == 1:
                start_all(b_first)
            else:
                back_copy(l - 1).start()
        return backs, own_terms

    def when_third(action, *copies):
        @pl.when(z_receives)
        def _():
            for c in copies:
                action(c)

    def z_last():
        up_last.wait_recv()
        down_last.wait_recv()

    def relay(first, last):
        first.wait_recv()
        last.start()

    def own_columns():
        arrive(own_x)
        neighbour_targets()

    actions = {
        "SF": lambda: start_all(f_first),
        "FR": lambda: relay_all(f_first, f_last), "BR": lambda: relay_all(b_first, b_last),
        "SYo": lambda: start(own_y), "RYo": lambda: arrive(own_y),
        "SXo": lambda: start(own_x), "RXo": own_columns,
        "SZ1": lambda: (up_first.start(), down_first.start()),
        "RU": lambda: relay(up_first, up_last), "RD": lambda: relay(down_first, down_last),
        "Z": z_last,
        "SYm": lambda: start(mate_y), "RYm": lambda: arrive(mate_y),
        "SXm": lambda: start(mate_x), "RXm": lambda: arrive(mate_x),
        "SZ2": lambda: start(z2_copies), "RZ2": lambda: arrive(z2_copies),
        "SYt": lambda: when_third(start, third_y), "RYt": lambda: when_third(arrive, third_y),
        "SXt": lambda: when_third(start, third_x), "RXt": lambda: when_third(arrive, third_x),
        "ES": send_extra, "ER": receive_extra,
    }
    pending = []

    def run_near():
        while pending:
            stride = pending[1] - pending[0] if len(pending) > 1 else 1
            count = 1
            while count < len(pending) and pending[count] - pending[count - 1] == stride:
                count += 1
            near(pending[0], stride, count)
            del pending[:count]

    for word in ORDER:
        if word[0] == "N":
            c = {"A": int(word[-1]) if word[-1].isdigit() else 0, "C": 4, "E": 5}[word[1]]
            pending.append("omt".index(word[2]) * 6 + c)
            continue
        run_near()
        if word == "SB":
            own_terms = first_back()
        elif word in actions:
            actions[word]()
        elif word[0] == "F":
            if int(word[1]) < depth:
                coefs = forward_step(int(word[1]), coefs)
        elif word[0] == "B":
            if int(word[1]) < depth:
                backs, own_terms = back_step(int(word[1]), own_terms)
    run_near()

    def pick_raster(g):
        total = res[0]
        for s in range(1, boxes):
            total = jnp.where(holds(g, s), res[s], total)
        return total

    for g in range(boxes):
        sums = pick_raster(g)
        far = dot(coefs[g], ll_out[g])
        out_ref[g, 0:32] = (
            fields_ref[g, 0:32].astype(F32) - (sums[0:32] + far[:, 0:128])
        ).astype(BF)
        out_ref[g, 32:64] = (
            fields_ref[g, 32:64].astype(F32) - (sums[32:64] + far[:, 128:256])
        ).astype(BF)
        far = dot(backs[g], ll_in[g])
        contrast = contrast_ref[g : g + 1, :]
        out_ref[boxes + g, 0:32] = (
            adj_ref[g, 0:32].astype(F32) - contrast * (sums[64:96] + far[:, 0:128])
        ).astype(BF)
        out_ref[boxes + g, 32:64] = (
            adj_ref[g, 32:64].astype(F32) - contrast * (sums[96:128] + far[:, 128:256])
        ).astype(BF)

    for l in range(1, depth):
        forward_copy(l).wait_send()
        back_copy(l).wait_send()
    for copy in f_first + f_last + b_first + b_last:
        copy.wait_send()
    up_first.wait_send()
    down_first.wait_send()
    up_last.wait_send()
    down_last.wait_send()
    sent(z2_copies)
    sent(own_y)
    sent(own_x)
    sent(mate_y)
    sent(mate_x)
    sent(extra_copies)

    @pl.when(z_receives)
    def _():
        sent(third_y)
        sent(third_x)


def body(fields, adjoint_in, contrast, coords, neighbours, partner_perm, leaf_in, leaf_out, mixing):
    boxes, parts, sides, points = fields.shape
    depth = mixing.shape[0]
    rank = leaf_in.shape[1]
    n_hi, n_lo = lax.axis_size("hi"), lax.axis_size("lo")
    scale = 1.0 / math.sqrt(27 * points)
    vmem = pl.BlockSpec(memory_space=pltpu.VMEM)
    smem = pl.BlockSpec(memory_space=pltpu.SMEM)
    away = pl.BlockSpec(memory_space=pl.ANY)
    flat = (boxes, parts * sides, points)
    copies = 2 * depth + 25
    level = (depth, boxes, sides, 2 * rank)
    inputs = (
        fields.reshape(flat), adjoint_in.reshape(flat), contrast, leaf_in, leaf_out, mixing,
    )
    out = pl.pallas_call(
        functools.partial(kernel, n_hi, n_lo, scale),
        out_shape=jax.ShapeDtypeStruct((2 * boxes,) + flat[1:], BF),
        in_specs=[smem, vmem] + [away] * 6,
        out_specs=vmem,
        scratch_shapes=[pltpu.VMEM(v.shape, v.dtype) for v in inputs]
        + [
            pltpu.VMEM((3, 4, 4, ROWS, points), BF),
            pltpu.VMEM((3, 16, 2 * points), BF),
            pltpu.VMEM((6, 4 * sides, 2 * points), F32),
            pltpu.VMEM((boxes, 2 * rank, 2 * points), BF),
            pltpu.VMEM((boxes, 2 * rank, 2 * points), BF),
            pltpu.VMEM((depth, boxes, 2 * rank, 4 * rank), BF),
            pltpu.VMEM(level, BF),
            pltpu.VMEM(level, BF),
            pltpu.VMEM(level, BF),
            pltpu.VMEM(level, BF),
            pltpu.VMEM((2, 2, ROWS, points), BF),
            pltpu.VMEM((2, 2) + level[2:], BF),
            pltpu.VMEM((2, 2) + level[2:], BF),
            pltpu.VMEM((boxes, 4 * sides, points), F32),
            pltpu.VMEM((2, 4 * sides, points), BF),
            pltpu.VMEM((2, 4 * sides, points), BF),
            pltpu.SemaphoreType.DMA((copies,)),
            pltpu.SemaphoreType.DMA((copies,)),
            pltpu.SemaphoreType.DMA((6,)),
        ]
        + [pltpu.VMEM(level[1:], BF)] * depth,
        compiler_params=pltpu.CompilerParams(
            collective_id=0, has_side_effects=True, vmem_limit_bytes=60 * 1024 * 1024
        ),
        name="operator",
    )(
        partner_perm.reshape(depth, boxes).T,
        coords.swapaxes(0, 1),
        *inputs,
    )
    return (out[:boxes].reshape(fields.shape), out[boxes:].reshape(fields.shape))


def solution(mesh):
    split = ("hi", "lo")
    in_specs = (
        P(split, None, None, None),
        P(split, None, None, None),
        P(split, None),
        P(split, None, None),
        P(split, None),
        P(None, split, None),
        P(split, None, None),
        P(split, None, None),
        P(None, split, None, None, None),
    )
    out_specs = (P(split, None, None, None), P(split, None, None, None))
    return jax.shard_map(body, mesh=mesh, in_specs=in_specs, out_specs=out_specs, check_vma=False)
```

```python
import functools
import math

import jax
import jax.numpy as jnp
import numpy as np
from jax import lax
from jax.experimental import pallas as pl
from jax.experimental.pallas import tpu as pltpu
from jax.sharding import PartitionSpec as P

WAVENUMBER = 9.0
SOFTENING = 0.1
MESH = pl.DeviceIdType.MESH
ROWS = 144
MAGIC = 12582912.0
BF = jnp.bfloat16
F32 = jnp.float32
NT = (((1,), (1,)), ((), ()))
TN = (((0,), (0,)), ((), ()))


ORDER = (
    "SF", "SB", "SZ1", "F0", "SYo", "B0", "F1", "RYo", "RU", "RD", "SXo", "NAo2", "B1", "F2",
    "NAo1", "Z", "SYm", "B2", "SZ2", "NAo0", "F3", "RXo", "NEo", "NAo3", "B3", "RZ2", "SYt", "RYm",
    "F4", "NCo", "SXm", "NEm", "NAm0", "B4", "F5", "RYt", "NAm3", "NEt", "SXt", "B5", "F6", "NAm2",
    "NAt1", "NAm1", "B6", "ES", "NAt3", "RXt", "RXm", "NAt2", "F7", "NCt", "NCm", "NAt0", "B7",
    "ER",
)


def fit(function, degree):
    nodes = 0.125 * (1.0 - np.cos(np.pi * (np.arange(400) + 0.5) / 400))
    poly = np.polynomial.chebyshev.Chebyshev.fit(nodes, function(nodes), degree, domain=[0, 0.25])
    return [float(c) for c in poly.convert(kind=np.polynomial.Polynomial).coef]


CYCLES = WAVENUMBER / (2 * math.pi)
COS_POLY = fit(lambda s: np.cos(2 * np.pi * np.sqrt(s)), 4)
SIN_POLY = fit(lambda s: np.sin(2 * np.pi * np.sqrt(s)) / np.sqrt(s), 3)


def horner(coefs, s):
    value = coefs[-1] * s + coefs[-2]
    for c in coefs[-3::-1]:
        value = value * s + c
    return value


def oscillation(squared, scale):
    w = squared * (CYCLES * CYCLES / 64.0) + CYCLES * CYCLES * SOFTENING * SOFTENING
    r = lax.rsqrt(w)
    y = w * r
    f = y - ((y + MAGIC) - MAGIC)
    s = f * f
    amp = scale * CYCLES
    real = horner([amp * c for c in COS_POLY], s) * r
    imag = horner([amp * c for c in SIN_POLY], s) * (f * r)
    return real.astype(BF), imag.astype(BF)


def spread(value, bits):
    total = 0
    for place, bit in enumerate(bits):
        total = total + (value // (1 << place)) % 2 * (1 << bit)
    return total


def dot(a, b, dims=None):
    if dims is None:
        return jnp.dot(a, b, preferred_element_type=F32)
    return lax.dot_general(a, b, dims, preferred_element_type=F32)


def kernel(
    n_hi, n_lo, scale,
    perm_ref, coords_ref, *refs,
):
    operands, refs = refs[:6], refs[6:]
    out_ref, *refs = refs
    (fields_ref, adj_ref, contrast_ref, lin_ref, lout_ref, mix_ref), refs = refs[:6], refs[6:]
    (
        grid, tgt, acc, ll_in, ll_out, blocks, fsend, bsend, brecv, carry, relays, res, exsend, exrecv,
        send_sem, recv_sem, load_sem, *frecv,
    ) = refs
    loads = [
        pltpu.make_async_copy(src, dst, load_sem.at[i])
        for i, (src, dst) in enumerate(
            zip(operands, (fields_ref, adj_ref, contrast_ref, lin_ref, lout_ref, mix_ref))
        )
    ]
    for load in loads:
        load.start()
    e = lax.axis_index("hi") * n_lo + lax.axis_index("lo")
    bits = (n_hi * n_lo).bit_length() - 1
    lo_bits = n_lo.bit_length() - 1
    levels = [b for b in range(bits) if b != lo_bits - 1]
    depth = len(levels)
    boxes = 4

    def where_is(device):
        return (device // n_lo, device % n_lo)

    def flip(bit):
        return e + (1 - 2 * ((e // (1 << bit)) % 2)) * (1 << bit)

    dims = []
    for d in range(3):
        own_bits = [t - 2 for t in range(2, bits + 2) if t % 3 == d]
        coord = 0
        for place, bit in enumerate(own_bits):
            coord = coord + (e // (1 << bit)) % 2 * (1 << place)
        rest = e - spread(coord, own_bits)
        dims.append((own_bits, coord, rest, 1 << len(own_bits)))

    def at(d, coordinate):
        own_bits, _, rest, _ = dims[d]
        return rest + spread(coordinate, own_bits)

    (_, xc, _, nx), (_, yc, _, ny), (_, zc, _, nz) = dims
    par = zc % 2
    mate = 2 - 2 * par
    third = 2 * par
    z_to = zc + 2 - 4 * par
    z_from = zc - 2 + 4 * par
    z_sends = jnp.logical_and(z_to >= 0, z_to < nz)
    z_receives = jnp.logical_and(z_from >= 0, z_from < nz)

    mirror = e // n_lo % 2
    xm = xc + mirror * (nx - 1 - 2 * xc)
    x_from, x_to = xc + 1 - 2 * mirror, xc - 1 + 2 * mirror
    imports, exports = xm < nx - 1, xm > 0
    far_edge, near_edge = (xm + 1) // nx, 1 - (xm + nx - 1) // nx

    def column(v):
        return v + mirror * (3 - 2 * v)

    ring_bits = list(range(lo_bits + 1, bits)) + [0]
    ring = 1 << len(ring_bits)
    zpos = 0
    for place, bit in enumerate(ring_bits):
        zpos = zpos + (e // (1 << bit)) % 2 * (1 << place)

    def on_ring(shift):
        return e - spread(zpos, ring_bits) + spread((zpos + ring + shift) % ring, ring_bits)

    def side(shift):
        return (zpos + ring + shift) % ring // (ring // 2)

    far_hop = ring // 2 - 1

    barrier = pltpu.get_barrier_semaphore()

    def greet(device):
        pl.semaphore_signal(barrier, inc=1, device_id=where_is(device), device_id_type=MESH)

    for bit in levels:
        greet(flip(bit))
    for shift in (far_hop, -far_hop, 1, -1):
        greet(on_ring(shift))
    others = []
    for d, n, c in ((0, nx, xc), (1, ny, yc)):
        others.append((c > 0, at(d, (c + n - 1) % n)))
        others.append((c < n - 1, at(d, (c + 1) % n)))
    others.append((z_sends, at(2, (z_to + nz) % nz)))
    others.append((z_receives, at(2, (z_from + nz) % nz)))
    for there, device in others:
        @pl.when(there)
        def _(device=device):
            greet(device)

    rank = lin_ref.shape[1]
    c = coords_ref[...].astype(F32)
    cells = jnp.floor(c)
    odd = cells - 2.0 * jnp.floor(0.5 * cells)
    raster = odd[0] + 2.0 * odd[1]
    c = c * 8.0
    norm = c[0] * c[0] + c[1] * c[1] + c[2] * c[2]
    high = jnp.floor(norm * (1.0 / 256.0)) * 256.0
    low = norm - high

    def holds(g, s):
        return raster[g : g + 1] == float(s)

    def pick(s, values):
        total = values[0]
        for g in range(1, boxes):
            total = jnp.where(holds(g, s), values[g], total)
        return total

    row = lax.broadcasted_iota(jnp.int32, (16, 128), 0)

    def stack(rows):
        value = jnp.zeros((16, 128), F32)
        for k, r in enumerate(rows):
            value = jnp.where(row == k, r, value)
        return value.astype(BF)

    one = jnp.ones((1, 128), F32)
    for s in range(boxes):
        x, y, z, h, w = (
            pick(s, [v[g : g + 1] for g in range(boxes)]) for v in (c[0], c[1], c[2], high, low)
        )
        grid[1, 1 + s // 2, 1 + s % 2, 128:144] = stack([x, y, z, h, w, one, one])
        tgt[column(1 + s % 2) - 1, :, 128 * (s // 2) : 128 * (s // 2) + 128] = stack(
            [-2.0 * x, -2.0 * y, -2.0 * z, one, one, h, w]
        )

    def double(ll, leaf, g):
        zero = jnp.zeros((rank, 128), BF)
        ll[g, 0:rank, 0:128] = leaf[g]
        ll[g, 0:rank, 128:256] = zero
        ll[g, rank : 2 * rank, 0:128] = zero
        ll[g, rank : 2 * rank, 128:256] = leaf[g]

    for load in loads[:4]:
        load.wait()
    weighted = []
    for g in range(boxes):
        double(ll_in, lin_ref, g)
        w = contrast_ref[g : g + 1, :] * fields_ref[g].astype(F32)
        weighted.append(w)
        lhs = jnp.concatenate([w[0:32], w[32:64]], axis=1).astype(BF)
        fsend[0, g] = dot(lhs, ll_in[g], NT).astype(BF)
    for s in range(boxes):
        place = (1, 1 + s // 2, 1 + s % 2)
        grid[place + (slice(0, 64),)] = pick(s, weighted).astype(BF)
        grid[place + (slice(64, 128),)] = pick(
            s, [adj_ref[g].astype(F32) for g in range(boxes)]
        ).astype(BF)

    def build(i, _):
        l, g = i // boxes, i % boxes
        zero = jnp.zeros((rank, rank), BF)
        for part in range(2):
            m = mix_ref[l, g, part]
            base = part * 128
            blocks[l, g, 0:rank, base : base + 128] = jnp.concatenate([m, zero], axis=1)
            blocks[l, g, rank : 2 * rank, base : base + 128] = jnp.concatenate([zero, m], axis=1)
        return 0

    def inverse(l, s):
        found = 0
        for j in range(1, boxes):
            found = found + jnp.where(perm_ref[j, l] == s, j, 0)
        return jnp.minimum(found, boxes - 1)

    def back_products(l, backs):
        own = []
        for g in range(boxes):
            both = dot(backs[g], blocks[l, g])
            own.append(both[:, 0:128])
            carry[l, g] = both[:, 128:256].astype(BF)
        for s in range(boxes):
            bsend[l, s] = carry[l, inverse(l, s)]
        return own

    def first_back():
        loads[4].wait()
        loads[5].wait()
        lax.fori_loop((depth - 1) * boxes, depth * boxes, build, 0)
        backs = []
        for g in range(boxes):
            double(ll_out, lout_ref, g)
            a = adj_ref[g]
            lhs = jnp.concatenate([a[0:32], a[32:64]], axis=1)
            backs.append(dot(lhs, ll_out[g], NT).astype(BF))
        own_terms = back_products(depth - 1, backs)
        back_copy(depth - 1).start()
        lax.fori_loop(0, (depth - 1) * boxes, build, 0)
        acc[...] = jnp.zeros_like(acc)
        return own_terms


    def remote(src, dst, sem, device):
        return pltpu.make_async_remote_copy(
            src_ref=src, dst_ref=dst, send_sem=send_sem.at[sem], recv_sem=recv_sem.at[sem],
            device_id=where_is(device), device_id_type=MESH,
        )

    def forward_copy(l):
        return remote(fsend.at[l], frecv[l], l, flip(levels[l]))

    def back_copy(l):
        return remote(bsend.at[l], brecv.at[l], depth + l, flip(levels[l]))

    first_sem = 2 * depth
    last_sem = first_sem + 14
    up_first = remote(
        grid.at[1, 1, pl.ds(1, 2)], relays.at[0], first_sem, on_ring(far_hop)
    )
    down_first = remote(
        grid.at[1, 2, pl.ds(1, 2)], relays.at[1], last_sem, on_ring(-far_hop)
    )
    up_last = remote(
        relays.at[0], grid.at[2 * side(-far_hop), 1, pl.ds(1, 2)], last_sem + 1, on_ring(1)
    )
    down_last = remote(
        relays.at[1], grid.at[2 * side(far_hop), 2, pl.ds(1, 2)], last_sem + 2, on_ring(-1)
    )
    z2 = remote(
        grid.at[mate, pl.ds(1, 2), pl.ds(1, 2)],
        grid.at[third, pl.ds(1, 2), pl.ds(1, 2)],
        first_sem + 1, at(2, (z_to + nz) % nz),
    )

    def y_copies(plane, kind):
        sem = first_sem + 2 + 4 * kind
        up = remote(
            grid.at[plane, 2, pl.ds(1, 2)], grid.at[plane, 0, pl.ds(1, 2)],
            sem, at(1, (yc + 1) % ny),
        )
        down = remote(
            grid.at[plane, 1, pl.ds(1, 2)], grid.at[plane, 3, pl.ds(1, 2)],
            sem + 1, at(1, (yc + ny - 1) % ny),
        )
        return ((up, yc < ny - 1, yc > 0), (down, yc > 0, yc < ny - 1))

    def x_copies(plane, kind):
        copy = remote(
            grid.at[plane, pl.ds(0, 4), 1 + mirror], grid.at[plane, pl.ds(0, 4), 3 - 3 * mirror],
            first_sem + 4 + 4 * kind, at(0, (x_to + nx) % nx),
        )
        return ((copy, exports, imports),)

    extra = remote(exsend, exrecv, first_sem + 5, at(0, (x_from + nx) % nx))
    extra_copies = ((extra, imports, exports),)

    def start(copies):
        for copy, sends, _ in copies:
            @pl.when(sends)
            def _(copy=copy):
                copy.start()

    def arrive(copies):
        for copy, _, receives in copies:
            @pl.when(receives)
            def _(copy=copy):
                copy.wait_recv()

    def sent(copies):
        for copy, sends, _ in copies:
            @pl.when(sends)
            def _(copy=copy):
                copy.wait_send()

    own_y, own_x = y_copies(1, 0), x_copies(1, 0)
    mate_y, mate_x = y_copies(mate, 1), x_copies(mate, 1)
    third_y, third_x = y_copies(third, 2), x_copies(third, 2)
    z2_copies = ((z2, z_sends, z_receives),)

    y_low, y_high = 1 - (yc + ny - 1) // ny, (yc + 1) // ny
    third_or_own = jnp.where(z_receives, third, 1)
    rows_of = [y_low, 1, 2, 3 - y_high]

    def near(first, stride, count):
        def step(i, _):
            j = first + stride * i
            k, c = j // 6, j % 6
            plane = 1 + k % 2 * (mate - 1) + k // 2 * (third_or_own - 1)
            goal = (c + 4) // 6 + c // 5
            source = 1 + c % 2 + 2 * (c // 4) - 2 * (c // 5)
            x = column(source - far_edge * (c // 4 - c // 5))
            weight = (1 + near_edge * (1 - (c + 4) // 5)).astype(F32)
            features = [grid[plane, y, x, 128:144] for y in rows_of]
            squared = dot(jnp.concatenate(features, axis=1), tgt[goal], TN)
            values = [grid[plane, y, x, 0:128] for y in rows_of]
            for ty in range(2):
                real, imag = oscillation(
                    squared[128 * ty : 128 * ty + 384, 128 * ty : 128 * ty + 128], scale
                )
                product = dot(
                    jnp.concatenate(values[ty : ty + 3], axis=1),
                    jnp.concatenate([real, imag], axis=1),
                )
                acc[3 * ty + goal] = acc[3 * ty + goal] + weight * product
            return 0

        lax.fori_loop(0, count, step, 0)

    def combine(a):
        ar, ai = a[:, 0:128], a[:, 128:256]
        return jnp.concatenate(
            [
                ar[0:32] - ai[32:64], ai[0:32] + ar[32:64],
                ar[64:96] + ai[96:128], ar[96:128] - ai[64:96],
            ],
            axis=0,
        )

    def neighbour_targets():
        for ty in range(2):
            f = grid[1, 1 + ty, 3 - 3 * mirror, 128:144].astype(F32)
            tgt[2, :, 128 * ty : 128 * ty + 128] = stack(
                [-2.0 * f[0:1], -2.0 * f[1:2], -2.0 * f[2:3], one, one, f[3:4], f[4:5]]
            )

    def send_extra():
        for ty in range(2):
            exsend[ty] = combine(acc[3 * ty + 2]).astype(BF)
        start(extra_copies)

    def receive_extra():
        for ty in range(2):
            for x in range(2):
                res[2 * ty + x] = combine(acc[3 * ty + column(1 + x) - 1])

        @pl.when(exports)
        def _():
            extra.wait_recv()
            for ty in range(2):
                mine = 2 * ty + mirror
                res[mine] = res[mine] + exrecv[ty].astype(F32)

    peers = depth + 4
    for there, _ in others:
        peers = peers + there.astype(jnp.int32)
    pl.semaphore_wait(barrier, peers)

    coefs = [fsend[0, g] for g in range(boxes)]

    def forward_step(i, coefs):
        mine = [dot(coefs[g], blocks[i, g, :, 0:128], NT) for g in range(boxes)]
        forward_copy(i).wait_recv()
        new = []
        for g in range(boxes):
            arrived = frecv[i][perm_ref[g, i]]
            c = (mine[g] + dot(arrived, blocks[i, g, :, 128:256], NT)).astype(BF)
            new.append(c)
            if i + 1 < depth:
                fsend[i + 1, g] = c
        if i + 1 < depth:
            forward_copy(i + 1).start()
        return new

    def back_step(i, own_terms):
        l = depth - 1 - i
        back_copy(l).wait_recv()
        backs = [(own_terms[g] + brecv[l, g].astype(F32)).astype(BF) for g in range(boxes)]
        if l > 0:
            own_terms = back_products(l - 1, backs)
            back_copy(l - 1).start()
        return backs, own_terms

    def when_third(action, *copies):
        @pl.when(z_receives)
        def _():
            for c in copies:
                action(c)

    def z_last():
        up_last.wait_recv()
        down_last.wait_recv()

    def relay(first, last):
        first.wait_recv()
        last.start()

    def own_columns():
        arrive(own_x)
        neighbour_targets()

    actions = {
        "SF": lambda: forward_copy(0).start(),
        "SYo": lambda: start(own_y), "RYo": lambda: arrive(own_y),
        "SXo": lambda: start(own_x), "RXo": own_columns,
        "SZ1": lambda: (up_first.start(), down_first.start()),
        "RU": lambda: relay(up_first, up_last), "RD": lambda: relay(down_first, down_last),
        "Z": z_last,
        "SYm": lambda: start(mate_y), "RYm": lambda: arrive(mate_y),
        "SXm": lambda: start(mate_x), "RXm": lambda: arrive(mate_x),
        "SZ2": lambda: start(z2_copies), "RZ2": lambda: arrive(z2_copies),
        "SYt": lambda: when_third(start, third_y), "RYt": lambda: when_third(arrive, third_y),
        "SXt": lambda: when_third(start, third_x), "RXt": lambda: when_third(arrive, third_x),
        "ES": send_extra, "ER": receive_extra,
    }
    pending = []

    def run_near():
        while pending:
            stride = pending[1] - pending[0] if len(pending) > 1 else 1
            count = 1
            while count < len(pending) and pending[count] - pending[count - 1] == stride:
                count += 1
            near(pending[0], stride, count)
            del pending[:count]

    for word in ORDER:
        if word[0] == "N":
            c = {"A": int(word[-1]) if word[-1].isdigit() else 0, "C": 4, "E": 5}[word[1]]
            pending.append("omt".index(word[2]) * 6 + c)
            continue
        run_near()
        if word == "SB":
            own_terms = first_back()
        elif word[0] == "F":
            if int(word[1]) < depth:
                coefs = forward_step(int(word[1]), coefs)
        elif word[0] == "B":
            if int(word[1]) < depth:
                backs, own_terms = back_step(int(word[1]), own_terms)
        else:
            actions[word]()
    run_near()

    def pick_raster(g):
        total = res[0]
        for s in range(1, boxes):
            total = jnp.where(holds(g, s), res[s], total)
        return total

    for g in range(boxes):
        sums = pick_raster(g)
        far = dot(coefs[g], ll_out[g])
        out_ref[g, 0:32] = (
            fields_ref[g, 0:32].astype(F32) - (sums[0:32] + far[:, 0:128])
        ).astype(BF)
        out_ref[g, 32:64] = (
            fields_ref[g, 32:64].astype(F32) - (sums[32:64] + far[:, 128:256])
        ).astype(BF)
        far = dot(backs[g], ll_in[g])
        contrast = contrast_ref[g : g + 1, :]
        out_ref[boxes + g, 0:32] = (
            adj_ref[g, 0:32].astype(F32) - contrast * (sums[64:96] + far[:, 0:128])
        ).astype(BF)
        out_ref[boxes + g, 32:64] = (
            adj_ref[g, 32:64].astype(F32) - contrast * (sums[96:128] + far[:, 128:256])
        ).astype(BF)

    for l in range(depth):
        forward_copy(l).wait_send()
        back_copy(l).wait_send()
    up_first.wait_send()
    down_first.wait_send()
    up_last.wait_send()
    down_last.wait_send()
    sent(z2_copies)
    sent(own_y)
    sent(own_x)
    sent(mate_y)
    sent(mate_x)
    sent(extra_copies)

    @pl.when(z_receives)
    def _():
        sent(third_y)
        sent(third_x)


def body(fields, adjoint_in, contrast, coords, neighbours, partner_perm, leaf_in, leaf_out, mixing):
    boxes, parts, sides, points = fields.shape
    depth = mixing.shape[0]
    rank = leaf_in.shape[1]
    n_hi, n_lo = lax.axis_size("hi"), lax.axis_size("lo")
    scale = 1.0 / math.sqrt(27 * points)
    vmem = pl.BlockSpec(memory_space=pltpu.VMEM)
    smem = pl.BlockSpec(memory_space=pltpu.SMEM)
    away = pl.BlockSpec(memory_space=pl.ANY)
    flat = (boxes, parts * sides, points)
    copies = 2 * depth + 17
    level = (depth, boxes, sides, 2 * rank)
    inputs = (
        fields.reshape(flat), adjoint_in.reshape(flat), contrast, leaf_in, leaf_out, mixing,
    )
    out = pl.pallas_call(
        functools.partial(kernel, n_hi, n_lo, scale),
        out_shape=jax.ShapeDtypeStruct((2 * boxes,) + flat[1:], BF),
        in_specs=[smem, vmem] + [away] * 6,
        out_specs=vmem,
        scratch_shapes=[pltpu.VMEM(v.shape, v.dtype) for v in inputs]
        + [
            pltpu.VMEM((3, 4, 4, ROWS, points), BF),
            pltpu.VMEM((3, 16, 2 * points), BF),
            pltpu.VMEM((6, 4 * sides, 2 * points), F32),
            pltpu.VMEM((boxes, 2 * rank, 2 * points), BF),
            pltpu.VMEM((boxes, 2 * rank, 2 * points), BF),
            pltpu.VMEM((depth, boxes, 2 * rank, 4 * rank), BF),
            pltpu.VMEM(level, BF),
            pltpu.VMEM(level, BF),
            pltpu.VMEM(level, BF),
            pltpu.VMEM(level, BF),
            pltpu.VMEM((2, 2, ROWS, points), BF),
            pltpu.VMEM((boxes, 4 * sides, points), F32),
            pltpu.VMEM((2, 4 * sides, points), BF),
            pltpu.VMEM((2, 4 * sides, points), BF),
            pltpu.SemaphoreType.DMA((copies,)),
            pltpu.SemaphoreType.DMA((copies,)),
            pltpu.SemaphoreType.DMA((6,)),
        ]
        + [pltpu.VMEM(level[1:], BF)] * depth,
        compiler_params=pltpu.CompilerParams(
            collective_id=0, has_side_effects=True, vmem_limit_bytes=60 * 1024 * 1024
        ),
        name="operator",
    )(
        partner_perm.reshape(depth, boxes).T,
        coords.swapaxes(0, 1),
        *inputs,
    )
    return (out[:boxes].reshape(fields.shape), out[boxes:].reshape(fields.shape))


def solution(mesh):
    split = ("hi", "lo")
    in_specs = (
        P(split, None, None, None),
        P(split, None, None, None),
        P(split, None),
        P(split, None, None),
        P(split, None),
        P(None, split, None),
        P(split, None, None),
        P(split, None, None),
        P(None, split, None, None, None),
    )
    out_specs = (P(split, None, None, None), P(split, None, None, None))
    return jax.shard_map(body, mesh=mesh, in_specs=in_specs, out_specs=out_specs, check_vma=False)
```

```python
import functools
import math

import jax
import jax.numpy as jnp
import numpy as np
from jax import lax
from jax.experimental import pallas as pl
from jax.experimental.pallas import tpu as pltpu
from jax.sharding import PartitionSpec as P

WAVENUMBER = 9.0
SOFTENING = 0.1
MESH = pl.DeviceIdType.MESH
ROWS = 144
MAGIC = 12582912.0
BF = jnp.bfloat16
F32 = jnp.float32
NT = (((1,), (1,)), ((), ()))
TN = (((0,), (0,)), ((), ()))


ORDER = (
    "SF", "SB", "SZ1", "P", "F0", "SYo", "B0", "F1", "RYo", "RU", "RD", "SXo", "NAo2", "B1", "F2",
    "NAo1", "Z", "SYm", "B2", "SZ2", "NAo0", "F3", "RXo", "NEo", "NAo3", "B3", "RZ2", "SYt", "RYm",
    "F4", "NCo", "SXm", "NEm", "NAm0", "B4", "F5", "RYt", "NAm3", "NEt", "SXt", "B5", "F6", "NAm2",
    "NAt1", "NAm1", "B6", "ES", "NAt3", "RXt", "RXm", "NAt2", "F7", "NCt", "NCm", "NAt0", "B7",
    "ER",
)


def fit(function, degree):
    nodes = 0.125 * (1.0 - np.cos(np.pi * (np.arange(400) + 0.5) / 400))
    poly = np.polynomial.chebyshev.Chebyshev.fit(nodes, function(nodes), degree, domain=[0, 0.25])
    return [float(c) for c in poly.convert(kind=np.polynomial.Polynomial).coef]


CYCLES = WAVENUMBER / (2 * math.pi)
COS_POLY = fit(lambda s: np.cos(2 * np.pi * np.sqrt(s)), 4)
SIN_POLY = fit(lambda s: np.sin(2 * np.pi * np.sqrt(s)) / np.sqrt(s), 3)


def horner(coefs, s):
    value = coefs[-1] * s + coefs[-2]
    for c in coefs[-3::-1]:
        value = value * s + c
    return value


def oscillation(squared, scale):
    w = squared * (CYCLES * CYCLES / 64.0) + CYCLES * CYCLES * SOFTENING * SOFTENING
    r = lax.rsqrt(w)
    y = w * r
    f = y - ((y + MAGIC) - MAGIC)
    s = f * f
    amp = scale * CYCLES
    real = horner([amp * c for c in COS_POLY], s) * r
    imag = horner([amp * c for c in SIN_POLY], s) * (f * r)
    return real.astype(BF), imag.astype(BF)


def spread(value, bits):
    total = 0
    for place, bit in enumerate(bits):
        total = total + (value // (1 << place)) % 2 * (1 << bit)
    return total


def dot(a, b, dims=None):
    if dims is None:
        return jnp.dot(a, b, preferred_element_type=F32)
    return lax.dot_general(a, b, dims, preferred_element_type=F32)


def kernel(
    n_hi, n_lo, scale,
    perm_ref, coords_ref, *refs,
):
    operands, refs = refs[:6], refs[6:]
    out_ref, *refs = refs
    (fields_ref, adj_ref, contrast_ref, lin_ref, lout_ref, mix_ref), refs = refs[:6], refs[6:]
    (
        grid, tgt, acc, ll_in, ll_out, blocks, fsend, bsend, brecv, carry, relays, res, exsend, exrecv,
        send_sem, recv_sem, load_sem, *frecv,
    ) = refs
    loads = [
        pltpu.make_async_copy(src, dst, load_sem.at[i])
        for i, (src, dst) in enumerate(
            zip(operands, (fields_ref, adj_ref, contrast_ref, lin_ref, lout_ref, mix_ref))
        )
    ]
    for load in loads:
        load.start()
    e = lax.axis_index("hi") * n_lo + lax.axis_index("lo")
    bits = (n_hi * n_lo).bit_length() - 1
    lo_bits = n_lo.bit_length() - 1
    levels = [b for b in range(bits) if b != lo_bits - 1]
    depth = len(levels)
    boxes = 4

    def where_is(device):
        return (device // n_lo, device % n_lo)

    def flip(bit):
        return e + (1 - 2 * ((e // (1 << bit)) % 2)) * (1 << bit)

    dims = []
    for d in range(3):
        own_bits = [t - 2 for t in range(2, bits + 2) if t % 3 == d]
        coord = 0
        for place, bit in enumerate(own_bits):
            coord = coord + (e // (1 << bit)) % 2 * (1 << place)
        rest = e - spread(coord, own_bits)
        dims.append((own_bits, coord, rest, 1 << len(own_bits)))

    def at(d, coordinate):
        own_bits, _, rest, _ = dims[d]
        return rest + spread(coordinate, own_bits)

    (_, xc, _, nx), (_, yc, _, ny), (_, zc, _, nz) = dims
    par = zc % 2
    mate = 2 - 2 * par
    third = 2 * par
    z_to = zc + 2 - 4 * par
    z_from = zc - 2 + 4 * par
    z_sends = jnp.logical_and(z_to >= 0, z_to < nz)
    z_receives = jnp.logical_and(z_from >= 0, z_from < nz)

    mirror = e // n_lo % 2
    xm = xc + mirror * (nx - 1 - 2 * xc)
    x_from, x_to = xc + 1 - 2 * mirror, xc - 1 + 2 * mirror
    imports, exports = xm < nx - 1, xm > 0
    far_edge, near_edge = (xm + 1) // nx, 1 - (xm + nx - 1) // nx

    def column(v):
        return v + mirror * (3 - 2 * v)

    ring_bits = list(range(lo_bits + 1, bits)) + [0]
    ring = 1 << len(ring_bits)
    zpos = 0
    for place, bit in enumerate(ring_bits):
        zpos = zpos + (e // (1 << bit)) % 2 * (1 << place)

    def on_ring(shift):
        return e - spread(zpos, ring_bits) + spread((zpos + ring + shift) % ring, ring_bits)

    def side(shift):
        return (zpos + ring + shift) % ring // (ring // 2)

    far_hop = ring // 2 - 1

    barrier = pltpu.get_barrier_semaphore()

    def greet(device):
        pl.semaphore_signal(barrier, inc=1, device_id=where_is(device), device_id_type=MESH)

    for bit in levels:
        greet(flip(bit))
    for shift in (far_hop, -far_hop, 1, -1):
        greet(on_ring(shift))
    others = []
    for d, n, c in ((0, nx, xc), (1, ny, yc)):
        others.append((c > 0, at(d, (c + n - 1) % n)))
        others.append((c < n - 1, at(d, (c + 1) % n)))
    others.append((z_sends, at(2, (z_to + nz) % nz)))
    others.append((z_receives, at(2, (z_from + nz) % nz)))
    for there, device in others:
        @pl.when(there)
        def _(device=device):
            greet(device)

    rank = lin_ref.shape[1]
    c = coords_ref[...].astype(F32)
    cells = jnp.floor(c)
    odd = cells - 2.0 * jnp.floor(0.5 * cells)
    raster = odd[0] + 2.0 * odd[1]
    c = c * 8.0
    norm = c[0] * c[0] + c[1] * c[1] + c[2] * c[2]
    high = jnp.floor(norm * (1.0 / 256.0)) * 256.0
    low = norm - high

    def holds(g, s):
        return raster[g : g + 1] == float(s)

    def pick(s, values):
        total = values[0]
        for g in range(1, boxes):
            total = jnp.where(holds(g, s), values[g], total)
        return total

    row = lax.broadcasted_iota(jnp.int32, (16, 128), 0)

    def stack(rows):
        value = jnp.zeros((16, 128), F32)
        for k, r in enumerate(rows):
            value = jnp.where(row == k, r, value)
        return value.astype(BF)

    one = jnp.ones((1, 128), F32)
    for s in range(boxes):
        x, y, z, h, w = (
            pick(s, [v[g : g + 1] for g in range(boxes)]) for v in (c[0], c[1], c[2], high, low)
        )
        grid[1, 1 + s // 2, 1 + s % 2, 128:144] = stack([x, y, z, h, w, one, one])
        tgt[column(1 + s % 2) - 1, :, 128 * (s // 2) : 128 * (s // 2) + 128] = stack(
            [-2.0 * x, -2.0 * y, -2.0 * z, one, one, h, w]
        )

    def double(ll, leaf, g):
        zero = jnp.zeros((rank, 128), BF)
        ll[g, 0:rank, 0:128] = leaf[g]
        ll[g, 0:rank, 128:256] = zero
        ll[g, rank : 2 * rank, 0:128] = zero
        ll[g, rank : 2 * rank, 128:256] = leaf[g]

    for load in loads[:4]:
        load.wait()
    weighted = []
    for g in range(boxes):
        double(ll_in, lin_ref, g)
        w = contrast_ref[g : g + 1, :] * fields_ref[g].astype(F32)
        weighted.append(w)
        lhs = jnp.concatenate([w[0:32], w[32:64]], axis=1).astype(BF)
        fsend[0, g] = dot(lhs, ll_in[g], NT).astype(BF)
    for s in range(boxes):
        place = (1, 1 + s // 2, 1 + s % 2)
        grid[place + (slice(0, 64),)] = pick(s, weighted).astype(BF)
        grid[place + (slice(64, 128),)] = pick(
            s, [adj_ref[g].astype(F32) for g in range(boxes)]
        ).astype(BF)

    def build(i, _):
        l, g = i // boxes, i % boxes
        zero = jnp.zeros((rank, rank), BF)
        for part in range(2):
            m = mix_ref[l, g, part]
            base = part * 128
            blocks[l, g, 0:rank, base : base + 128] = jnp.concatenate([m, zero], axis=1)
            blocks[l, g, rank : 2 * rank, base : base + 128] = jnp.concatenate([zero, m], axis=1)
        return 0

    def inverse(l, s):
        found = 0
        for j in range(1, boxes):
            found = found + jnp.where(perm_ref[j, l] == s, j, 0)
        return jnp.minimum(found, boxes - 1)

    def back_products(l, backs):
        own = []
        for g in range(boxes):
            both = dot(backs[g], blocks[l, g])
            own.append(both[:, 0:128])
            carry[l, g] = both[:, 128:256].astype(BF)
        for s in range(boxes):
            bsend[l, s] = carry[l, inverse(l, s)]
        return own

    def first_back():
        loads[4].wait()
        loads[5].wait()
        lax.fori_loop((depth - 1) * boxes, depth * boxes, build, 0, unroll=boxes)
        backs = []
        for g in range(boxes):
            double(ll_out, lout_ref, g)
            a = adj_ref[g]
            lhs = jnp.concatenate([a[0:32], a[32:64]], axis=1)
            backs.append(dot(lhs, ll_out[g], NT).astype(BF))
        own_terms = back_products(depth - 1, backs)
        back_copy(depth - 1).start()
        return own_terms

    def other_blocks():
        lax.fori_loop(0, (depth - 1) * boxes, build, 0, unroll=boxes)
        acc[...] = jnp.zeros_like(acc)


    def remote(src, dst, sem, device):
        return pltpu.make_async_remote_copy(
            src_ref=src, dst_ref=dst, send_sem=send_sem.at[sem], recv_sem=recv_sem.at[sem],
            device_id=where_is(device), device_id_type=MESH,
        )

    def forward_copy(l):
        return remote(fsend.at[l], frecv[l], l, flip(levels[l]))

    def back_copy(l):
        return remote(bsend.at[l], brecv.at[l], depth + l, flip(levels[l]))

    first_sem = 2 * depth
    last_sem = first_sem + 14
    up_first = remote(
        grid.at[1, 1, pl.ds(1, 2)], relays.at[0], first_sem, on_ring(far_hop)
    )
    down_first = remote(
        grid.at[1, 2, pl.ds(1, 2)], relays.at[1], last_sem, on_ring(-far_hop)
    )
    up_last = remote(
        relays.at[0], grid.at[2 * side(-far_hop), 1, pl.ds(1, 2)], last_sem + 1, on_ring(1)
    )
    down_last = remote(
        relays.at[1], grid.at[2 * side(far_hop), 2, pl.ds(1, 2)], last_sem + 2, on_ring(-1)
    )
    z2 = remote(
        grid.at[mate, pl.ds(1, 2), pl.ds(1, 2)],
        grid.at[third, pl.ds(1, 2), pl.ds(1, 2)],
        first_sem + 1, at(2, (z_to + nz) % nz),
    )

    def y_copies(plane, kind):
        sem = first_sem + 2 + 4 * kind
        up = remote(
            grid.at[plane, 2, pl.ds(1, 2)], grid.at[plane, 0, pl.ds(1, 2)],
            sem, at(1, (yc + 1) % ny),
        )
        down = remote(
            grid.at[plane, 1, pl.ds(1, 2)], grid.at[plane, 3, pl.ds(1, 2)],
            sem + 1, at(1, (yc + ny - 1) % ny),
        )
        return ((up, yc < ny - 1, yc > 0), (down, yc > 0, yc < ny - 1))

    def x_copies(plane, kind):
        copy = remote(
            grid.at[plane, pl.ds(0, 4), 1 + mirror], grid.at[plane, pl.ds(0, 4), 3 - 3 * mirror],
            first_sem + 4 + 4 * kind, at(0, (x_to + nx) % nx),
        )
        return ((copy, exports, imports),)

    extra = remote(exsend, exrecv, first_sem + 5, at(0, (x_from + nx) % nx))
    extra_copies = ((extra, imports, exports),)

    def start(copies):
        for copy, sends, _ in copies:
            @pl.when(sends)
            def _(copy=copy):
                copy.start()

    def arrive(copies):
        for copy, _, receives in copies:
            @pl.when(receives)
            def _(copy=copy):
                copy.wait_recv()

    def sent(copies):
        for copy, sends, _ in copies:
            @pl.when(sends)
            def _(copy=copy):
                copy.wait_send()

    own_y, own_x = y_copies(1, 0), x_copies(1, 0)
    mate_y, mate_x = y_copies(mate, 1), x_copies(mate, 1)
    third_y, third_x = y_copies(third, 2), x_copies(third, 2)
    z2_copies = ((z2, z_sends, z_receives),)

    y_low, y_high = 1 - (yc + ny - 1) // ny, (yc + 1) // ny
    third_or_own = jnp.where(z_receives, third, 1)
    rows_of = [y_low, 1, 2, 3 - y_high]

    def near(first, stride, count):
        def step(i, _):
            j = first + stride * i
            k, c = j // 6, j % 6
            plane = 1 + k % 2 * (mate - 1) + k // 2 * (third_or_own - 1)
            goal = (c + 4) // 6 + c // 5
            source = 1 + c % 2 + 2 * (c // 4) - 2 * (c // 5)
            x = column(source - far_edge * (c // 4 - c // 5))
            weight = (1 + near_edge * (1 - (c + 4) // 5)).astype(F32)
            features = [grid[plane, y, x, 128:144] for y in rows_of]
            squared = dot(jnp.concatenate(features, axis=1), tgt[goal], TN)
            values = [grid[plane, y, x, 0:128] for y in rows_of]
            for ty in range(2):
                real, imag = oscillation(
                    squared[128 * ty : 128 * ty + 384, 128 * ty : 128 * ty + 128], scale
                )
                product = dot(
                    jnp.concatenate(values[ty : ty + 3], axis=1),
                    jnp.concatenate([real, imag], axis=1),
                )
                acc[3 * ty + goal] = acc[3 * ty + goal] + weight * product
            return 0

        lax.fori_loop(0, count, step, 0)

    def combine(a):
        ar, ai = a[:, 0:128], a[:, 128:256]
        return jnp.concatenate(
            [
                ar[0:32] - ai[32:64], ai[0:32] + ar[32:64],
                ar[64:96] + ai[96:128], ar[96:128] - ai[64:96],
            ],
            axis=0,
        )

    def neighbour_targets():
        for ty in range(2):
            f = grid[1, 1 + ty, 3 - 3 * mirror, 128:144].astype(F32)
            tgt[2, :, 128 * ty : 128 * ty + 128] = stack(
                [-2.0 * f[0:1], -2.0 * f[1:2], -2.0 * f[2:3], one, one, f[3:4], f[4:5]]
            )

    def send_extra():
        for ty in range(2):
            exsend[ty] = combine(acc[3 * ty + 2]).astype(BF)
        start(extra_copies)

    def receive_extra():
        for ty in range(2):
            for x in range(2):
                res[2 * ty + x] = combine(acc[3 * ty + column(1 + x) - 1])

        @pl.when(exports)
        def _():
            extra.wait_recv()
            for ty in range(2):
                mine = 2 * ty + mirror
                res[mine] = res[mine] + exrecv[ty].astype(F32)

    peers = depth + 4
    for there, _ in others:
        peers = peers + there.astype(jnp.int32)
    pl.semaphore_wait(barrier, peers)

    coefs = [fsend[0, g] for g in range(boxes)]

    def forward_step(i, coefs):
        mine = [dot(coefs[g], blocks[i, g, :, 0:128], NT) for g in range(boxes)]
        forward_copy(i).wait_recv()
        new = []
        for g in range(boxes):
            arrived = frecv[i][perm_ref[g, i]]
            c = (mine[g] + dot(arrived, blocks[i, g, :, 128:256], NT)).astype(BF)
            new.append(c)
            if i + 1 < depth:
                fsend[i + 1, g] = c
        if i + 1 < depth:
            forward_copy(i + 1).start()
        return new

    def back_step(i, own_terms):
        l = depth - 1 - i
        back_copy(l).wait_recv()
        backs = [(own_terms[g] + brecv[l, g].astype(F32)).astype(BF) for g in range(boxes)]
        if l > 0:
            own_terms = back_products(l - 1, backs)
            back_copy(l - 1).start()
        return backs, own_terms

    def when_third(action, *copies):
        @pl.when(z_receives)
        def _():
            for c in copies:
                action(c)

    def z_last():
        up_last.wait_recv()
        down_last.wait_recv()

    def relay(first, last):
        first.wait_recv()
        last.start()

    def own_columns():
        arrive(own_x)
        neighbour_targets()

    actions = {
        "SF": lambda: forward_copy(0).start(),
        "SYo": lambda: start(own_y), "RYo": lambda: arrive(own_y),
        "SXo": lambda: start(own_x), "RXo": own_columns,
        "SZ1": lambda: (up_first.start(), down_first.start()),
        "RU": lambda: relay(up_first, up_last), "RD": lambda: relay(down_first, down_last),
        "Z": z_last,
        "SYm": lambda: start(mate_y), "RYm": lambda: arrive(mate_y),
        "SXm": lambda: start(mate_x), "RXm": lambda: arrive(mate_x),
        "SZ2": lambda: start(z2_copies), "RZ2": lambda: arrive(z2_copies),
        "SYt": lambda: when_third(start, third_y), "RYt": lambda: when_third(arrive, third_y),
        "SXt": lambda: when_third(start, third_x), "RXt": lambda: when_third(arrive, third_x),
        "ES": send_extra, "ER": receive_extra, "P": other_blocks,
    }
    pending = []

    def run_near():
        while pending:
            stride = pending[1] - pending[0] if len(pending) > 1 else 1
            count = 1
            while count < len(pending) and pending[count] - pending[count - 1] == stride:
                count += 1
            near(pending[0], stride, count)
            del pending[:count]

    for word in ORDER:
        if word[0] == "N":
            c = {"A": int(word[-1]) if word[-1].isdigit() else 0, "C": 4, "E": 5}[word[1]]
            pending.append("omt".index(word[2]) * 6 + c)
            continue
        run_near()
        if word == "SB":
            own_terms = first_back()
        elif word[0] == "F":
            if int(word[1]) < depth:
                coefs = forward_step(int(word[1]), coefs)
        elif word[0] == "B":
            if int(word[1]) < depth:
                backs, own_terms = back_step(int(word[1]), own_terms)
        else:
            actions[word]()
    run_near()

    def pick_raster(g):
        total = res[0]
        for s in range(1, boxes):
            total = jnp.where(holds(g, s), res[s], total)
        return total

    for g in range(boxes):
        sums = pick_raster(g)
        far = dot(coefs[g], ll_out[g])
        out_ref[g, 0:32] = (
            fields_ref[g, 0:32].astype(F32) - (sums[0:32] + far[:, 0:128])
        ).astype(BF)
        out_ref[g, 32:64] = (
            fields_ref[g, 32:64].astype(F32) - (sums[32:64] + far[:, 128:256])
        ).astype(BF)
        far = dot(backs[g], ll_in[g])
        contrast = contrast_ref[g : g + 1, :]
        out_ref[boxes + g, 0:32] = (
            adj_ref[g, 0:32].astype(F32) - contrast * (sums[64:96] + far[:, 0:128])
        ).astype(BF)
        out_ref[boxes + g, 32:64] = (
            adj_ref[g, 32:64].astype(F32) - contrast * (sums[96:128] + far[:, 128:256])
        ).astype(BF)

    for l in range(depth):
        forward_copy(l).wait_send()
        back_copy(l).wait_send()
    up_first.wait_send()
    down_first.wait_send()
    up_last.wait_send()
    down_last.wait_send()
    sent(z2_copies)
    sent(own_y)
    sent(own_x)
    sent(mate_y)
    sent(mate_x)
    sent(extra_copies)

    @pl.when(z_receives)
    def _():
        sent(third_y)
        sent(third_x)


def body(fields, adjoint_in, contrast, coords, neighbours, partner_perm, leaf_in, leaf_out, mixing):
    boxes, parts, sides, points = fields.shape
    depth = mixing.shape[0]
    rank = leaf_in.shape[1]
    n_hi, n_lo = lax.axis_size("hi"), lax.axis_size("lo")
    scale = 1.0 / math.sqrt(27 * points)
    vmem = pl.BlockSpec(memory_space=pltpu.VMEM)
    smem = pl.BlockSpec(memory_space=pltpu.SMEM)
    away = pl.BlockSpec(memory_space=pl.ANY)
    flat = (boxes, parts * sides, points)
    copies = 2 * depth + 17
    level = (depth, boxes, sides, 2 * rank)
    inputs = (
        fields.reshape(flat), adjoint_in.reshape(flat), contrast, leaf_in, leaf_out, mixing,
    )
    out = pl.pallas_call(
        functools.partial(kernel, n_hi, n_lo, scale),
        out_shape=jax.ShapeDtypeStruct((2 * boxes,) + flat[1:], BF),
        in_specs=[smem, vmem] + [away] * 6,
        out_specs=vmem,
        scratch_shapes=[pltpu.VMEM(v.shape, v.dtype) for v in inputs]
        + [
            pltpu.VMEM((3, 4, 4, ROWS, points), BF),
            pltpu.VMEM((3, 16, 2 * points), BF),
            pltpu.VMEM((6, 4 * sides, 2 * points), F32),
            pltpu.VMEM((boxes, 2 * rank, 2 * points), BF),
            pltpu.VMEM((boxes, 2 * rank, 2 * points), BF),
            pltpu.VMEM((depth, boxes, 2 * rank, 4 * rank), BF),
            pltpu.VMEM(level, BF),
            pltpu.VMEM(level, BF),
            pltpu.VMEM(level, BF),
            pltpu.VMEM(level, BF),
            pltpu.VMEM((2, 2, ROWS, points), BF),
            pltpu.VMEM((boxes, 4 * sides, points), F32),
            pltpu.VMEM((2, 4 * sides, points), BF),
            pltpu.VMEM((2, 4 * sides, points), BF),
            pltpu.SemaphoreType.DMA((copies,)),
            pltpu.SemaphoreType.DMA((copies,)),
            pltpu.SemaphoreType.DMA((6,)),
        ]
        + [pltpu.VMEM(level[1:], BF)] * depth,
        compiler_params=pltpu.CompilerParams(
            collective_id=0, has_side_effects=True, vmem_limit_bytes=60 * 1024 * 1024
        ),
        name="operator",
    )(
        partner_perm.reshape(depth, boxes).T,
        coords.swapaxes(0, 1),
        *inputs,
    )
    return (out[:boxes].reshape(fields.shape), out[boxes:].reshape(fields.shape))


def solution(mesh):
    split = ("hi", "lo")
    in_specs = (
        P(split, None, None, None),
        P(split, None, None, None),
        P(split, None),
        P(split, None, None),
        P(split, None),
        P(None, split, None),
        P(split, None, None),
        P(split, None, None),
        P(None, split, None, None, None),
    )
    out_specs = (P(split, None, None, None), P(split, None, None, None))
    return jax.shard_map(body, mesh=mesh, in_specs=in_specs, out_specs=out_specs, check_vma=False)
```
